128 devices in a mesh: kv: 16 (over y, z), tp: 8 (over x, core).
Axes of the slice: x: 4, y: 4, z: 4, core: 2. Of those that a mesh axis runs over, the one named last changes fastest.
Arguments:
- states: bfloat16 [128, 8192], P(None, 'kv'), may hold values from -64 to 64
- first_gain: float32 [8192], P('kv'), may hold values from 0.5 to 1.5
- input_weight: bfloat16 [8192, 8, 1280], P('kv', 'tp'), may hold values from -0.0625 to 0.0625
- input_bias: bfloat16 [8, 1280], P('tp'), may hold values from -64 to 64
- output_weight: bfloat16 [8, 1024, 8192], P('tp', None, 'kv'), may hold values from -0.5 to 0.5
- second_gain: float32 [8192], P('kv'), may hold values from 0.5 to 1.5
- expand_weight: bfloat16 [8192, 2, 29568], P('kv', None, 'tp'), may hold values from -0.0625 to 0.0625
- shrink_weight: bfloat16 [29568, 8192], P('tp', 'kv'), may hold values from -0.03125 to 0.03125
- prompt_cache: bfloat16 [2, 8, 256, 512, 128], P(None, 'tp', 'kv'), may hold values from -64 to 64
- tail_cache: bfloat16 [2, 128, 512, 8, 128], P(None, 'kv', None, 'tp'), may hold values from -64 to 64
- tail_length: int32 [128], P('kv'), may hold values from 1 to 509, as said below
- block_index: int32 [128, 8, 16, 2], P('kv', 'tp'), may hold values from 0 to 15, as said below
- block_count: int32 [128, 8, 16], P('kv', 'tp'), may hold values from 0 to 2, as said below
Outputs:
- layer_out: bfloat16 [128, 8192], P(None, 'kv')
- new_cache: bfloat16 [2, 128, 3, 8, 128], P(None, 'kv', None, 'tp')
The draws below stay inside these ranges and needn't reach their ends.
Inputs may be any that keep to these rules, and one draw needn't show every extreme that they name: `block_index`: local block numbers at the owner; for each row and key-value head the blocks named (entries before the count) are distinct. Entries at or past the count are valid numbers that carry no weight. `block_count`: for each row and key-value head the counts over owners sum to 12, and some owner holds 2 of the blocks. `tail_length`: some row has the largest value.
All inputs are finite; a program needn't handle non-finite values.
Results may differ from the reference program's by a relative error of at most 0.03.
Values may be sent and summed in bfloat16 or wider, within the bound.
A program may use at most 128 MiB of HBM per device.

```python
import jax
import jax.numpy as jnp
from jax import lax

D = 8192
KVH = 8
GQ = 8
HD = 128
FF = 29568
BLK_DEV = 16
BLOCK = 512
NSEL = 12
CAP = 2
TAIL = 512
STEPS = 3
ROWS = 128
NBLK = 256
N_KV = 16


def block_tables(key):
    first, second, third, fourth, fifth = jax.random.split(key, 5)
    slots = N_KV * CAP
    favored = jax.random.randint(first, (KVH,), 0, N_KV)
    coin = jax.random.randint(second, (ROWS, KVH), 0, 2)
    other = jax.random.randint(third, (ROWS, KVH), 0, N_KV)
    home = jnp.where(coin == 1, favored[None, :], other)
    owner_of = jnp.arange(slots, dtype=jnp.int32) // CAP
    scores = jax.random.randint(fourth, (ROWS, KVH, slots), 0, 2 ** 20) * slots + jnp.arange(slots, dtype=jnp.int32)
    scores = jnp.where(owner_of[None, None, :] == home[:, :, None], scores + 2 ** 27, scores)
    chosen_values, chosen_places = lax.top_k(scores, NSEL)
    chosen = scores >= chosen_values[:, :, NSEL - 1:NSEL]
    counts = jnp.sum(chosen.reshape(ROWS, KVH, N_KV, CAP).astype(jnp.int32), axis=3)
    order = jax.random.randint(fifth, (ROWS, KVH, N_KV, BLK_DEV), 0, 2 ** 16) * BLK_DEV + jnp.arange(BLK_DEV, dtype=jnp.int32)
    index = jnp.argsort(order, axis=3)[:, :, :, :CAP].astype(jnp.int32)
    return (index, counts.astype(jnp.int32))


def draw_block_index(key, part):
    index, counts = block_tables(key)
    return index


def draw_block_count(key, part):
    index, counts = block_tables(key)
    return counts


def draw_tail_length(key, part):
    key = jax.random.fold_in(key, 7)
    first, second = jax.random.split(key)
    values = jax.random.randint(first, (ROWS,), 1, TAIL - STEPS + 1)
    chosen = jax.random.randint(second, (), 0, ROWS)
    return jnp.where(jnp.arange(ROWS, dtype=jnp.int32) == chosen, TAIL - STEPS, values).astype(jnp.int32)


def draw_states(key, part):
    key = jax.random.fold_in(key, 11)
    first = jax.random.fold_in(key, 0)
    column = jnp.arange(D, dtype=jnp.float32) / D
    base = jax.random.normal(first, (ROWS, D), jnp.float32)
    scale = 3.0 ** (0.5 * column)
    return jnp.clip(base * scale[None, :], -60.0, 60.0).astype(jnp.bfloat16)


def draw_input_bias(key, part):
    key = jax.random.fold_in(key, 13)
    first = jax.random.fold_in(key, 0)
    width = (GQ + 2) * HD
    values = 0.5 * jax.random.normal(first, (KVH, width), jnp.float32)
    return values.astype(jnp.bfloat16)


def cache_values(key, shape):
    first = jax.random.fold_in(key, 0)
    values = jax.random.normal(first, shape, jnp.float32)
    return values.astype(jnp.bfloat16)


def draw_prompt_cache(key, part):
    key = jax.random.fold_in(key, 17)
    return cache_values(key, (2, KVH, NBLK, BLOCK, HD))


def draw_tail_cache(key, part):
    key = jax.random.fold_in(key, 19)
    return cache_values(key, (2, ROWS, TAIL, KVH, HD))


def steps_of(key, shape, shards, least, largest):
    level = 1.0
    for position, blocks in shards:
        steps = jax.random.uniform(jax.random.fold_in(jax.random.fold_in(key, 6), position), (blocks,), jnp.float32, least / len(shards), largest / len(shards))
        level = level * jnp.repeat(jnp.exp(steps), shape[position] // blocks).reshape((-1,) + (1,) * (len(shape) - 1 - position))
    return level


def bell_draw(own_key, dims, spread, reach, shards=(), kind=jnp.bfloat16):
    entries = jax.random.normal(own_key, dims, jnp.float32) * spread
    if len(shards) > 0:
        entries = steps_of(own_key, dims, shards, -0.22, 0.18) * entries
    return jnp.clip(entries, min=-reach, max=reach).astype(kind)


def setup_inputs(seed: int = 0) -> dict:
    key_of = jax.random.split(jax.random.key(seed), 14)
    states = draw_states(jax.random.fold_in(key_of[13], 71), 0)
    first_gain = jnp.clip(1.0 + 0.1 * jax.random.normal(key_of[1], (D,), jnp.float32), 0.5, 1.5)
    input_weight = bell_draw(key_of[2], (D, KVH, (GQ + 2) * HD), D ** -0.5, 0.0625, ((0, 16), (1, 8)))
    input_bias = draw_input_bias(jax.random.fold_in(key_of[13], 71), 0)
    output_weight = bell_draw(key_of[4], (KVH, GQ * HD, D), HD ** -0.5, 0.5, ((0, 8), (2, 16)))
    second_gain = jnp.clip(1.0 + 0.1 * jax.random.normal(key_of[5], (D,), jnp.float32), 0.5, 1.5)
    expand_weight = bell_draw(key_of[6], (D, 2, FF), D ** -0.5, 0.0625, ((0, 16), (2, 8)))
    shrink_weight = bell_draw(key_of[7], (FF, D), FF ** -0.5, 0.03125, ((0, 8), (1, 16)))
    prompt_cache = draw_prompt_cache(jax.random.fold_in(key_of[13], 71), 0)
    tail_cache = draw_tail_cache(jax.random.fold_in(key_of[13], 71), 0)
    tail_length = draw_tail_length(jax.random.fold_in(key_of[13], 71), 0)
    block_index = draw_block_index(jax.random.fold_in(key_of[13], 71), 0)
    block_count = draw_block_count(jax.random.fold_in(key_of[13], 71), 0)
    return dict(states=states, first_gain=first_gain, input_weight=input_weight, input_bias=input_bias, output_weight=output_weight, second_gain=second_gain, expand_weight=expand_weight, shrink_weight=shrink_weight, prompt_cache=prompt_cache, tail_cache=tail_cache, tail_length=tail_length, block_index=block_index, block_count=block_count)


epsilon = 1e-06
very_low = -1e+30

def rms_scale(values, gain):
    wide = values.astype(jnp.float32)
    squares = lax.optimization_barrier(jnp.sum(wide * wide, axis=1))
    factor = lax.rsqrt(squares / D + epsilon)
    return (wide * factor[:, None] * gain[None, :]).astype(jnp.bfloat16)

def round_trip(values):
    narrow = lax.optimization_barrier(values.astype(jnp.bfloat16))
    return narrow.astype(jnp.float32)

def row_attention(query, index_row, count_row, tail_keys, tail_values, tail_live, fresh_keys, fresh_values, prompt_cache):
    scale = HD ** (-0.5)
    owners = jnp.arange(N_KV, dtype=jnp.int32)
    global_index = owners[None, :, None] * BLK_DEV + index_row
    heads = jnp.arange(KVH, dtype=jnp.int32)[:, None, None]
    keys = prompt_cache[0][heads, global_index].astype(jnp.float32)
    values = prompt_cache[1][heads, global_index].astype(jnp.float32)
    wide_query = query.astype(jnp.float32)
    scores = jnp.einsum('gjd,gocbd->gjocb', wide_query, keys) * scale
    live = jnp.arange(CAP, dtype=jnp.int32)[None, None, :] < count_row[:, :, None]
    live = live[:, None, :, :, None]
    peak = lax.optimization_barrier(jnp.max(jnp.where(live, scores, very_low), axis=(3, 4)))
    weights = jnp.where(live, jnp.exp(scores - peak[:, :, :, None, None]), 0.0)
    totals = lax.optimization_barrier(jnp.sum(weights, axis=(3, 4)))
    partial_value = jnp.einsum('gjocb,gocbd->gjod', round_trip(weights), values)
    all_keys = jnp.concatenate([tail_keys, fresh_keys], axis=0).astype(jnp.float32)
    all_values = jnp.concatenate([tail_values, fresh_values], axis=0).astype(jnp.float32)
    tail_scores = jnp.einsum('gjd,tgd->gjt', wide_query, all_keys) * scale
    positions = jnp.arange(all_keys.shape[0], dtype=jnp.int32)
    tail_mask = jnp.logical_or(positions < tail_live, positions >= TAIL)[None, None, :]
    tail_peak = lax.optimization_barrier(jnp.max(jnp.where(tail_mask, tail_scores, very_low), axis=2))
    tail_weights = jnp.where(tail_mask, jnp.exp(tail_scores - tail_peak[:, :, None]), 0.0)
    tail_total = lax.optimization_barrier(jnp.sum(tail_weights, axis=2))
    tail_part = jnp.einsum('gjt,tgd->gjd', round_trip(tail_weights), all_values)
    top = jnp.maximum(lax.optimization_barrier(jnp.max(peak, axis=2)), tail_peak)
    ratio = jnp.exp(peak - top[:, :, None])
    tail_ratio = jnp.exp(tail_peak - top)
    total = lax.optimization_barrier(jnp.sum(totals * ratio, axis=2)) + tail_total * tail_ratio
    summed = lax.optimization_barrier(jnp.sum(partial_value * ratio[:, :, :, None], axis=2)) + tail_part * tail_ratio[:, :, None]
    return (summed / total[:, :, None]).astype(jnp.bfloat16)

def reference(states, first_gain, input_weight, input_bias, output_weight, second_gain, expand_weight, shrink_weight, prompt_cache, tail_cache, tail_length, block_index, block_count):
    key_list = []
    value_list = []
    flat_input = input_weight.reshape(D, KVH * (GQ + 2) * HD)
    flat_bias = input_bias.reshape(KVH * (GQ + 2) * HD).astype(jnp.float32)
    flat_output = output_weight.reshape(KVH * GQ * HD, D)
    flat_expand = expand_weight.reshape(D, 2 * FF)
    for step in range(STEPS):
        normed = rms_scale(states, first_gain)
        projected = jnp.dot(normed, flat_input, preferred_element_type=jnp.float32) + flat_bias[None, :]
        projected = projected.astype(jnp.bfloat16).reshape(ROWS, KVH, GQ + 2, HD)
        query = projected[:, :, :GQ]
        key_list.append(projected[:, :, GQ])
        value_list.append(projected[:, :, GQ + 1])
        fresh_keys = jnp.stack(key_list, axis=1)
        fresh_values = jnp.stack(value_list, axis=1)

        def one_row(items):
            return row_attention(items[0], items[1], items[2], items[3], items[4], items[5], items[6], items[7], prompt_cache)
        attended = lax.map(one_row, (query, block_index, block_count, tail_cache[0], tail_cache[1], tail_length, fresh_keys, fresh_values))
        mixed = jnp.dot(attended.reshape(ROWS, KVH * GQ * HD), flat_output, preferred_element_type=jnp.float32)
        middle = (states.astype(jnp.float32) + mixed).astype(jnp.bfloat16)
        normed_mid = rms_scale(middle, second_gain)
        expanded = jnp.dot(normed_mid, flat_expand, preferred_element_type=jnp.float32)
        activated = (jax.nn.silu(expanded[:, :FF]) * expanded[:, FF:]).astype(jnp.bfloat16)
        shrunk = jnp.dot(activated, shrink_weight, preferred_element_type=jnp.float32)
        states = (middle.astype(jnp.float32) + shrunk).astype(jnp.bfloat16)
    new_cache = jnp.stack([jnp.stack(key_list, axis=1), jnp.stack(value_list, axis=1)], axis=0)
    return (states, new_cache)
```

```python
import functools

import jax
import jax.numpy as jnp
from jax import lax
from jax.experimental import pallas as pl
from jax.experimental.pallas import tpu as pltpu
from jax.sharding import PartitionSpec as P

D = 8192
STEPS = 3
ROWS = 128
LOC = 8
HEADS = 8
HD = 128
QW = HEADS * HD
PW = QW + 2 * HD
BLOCKS = 16
BLOCK = 512
TAIL = 512
FF = 3696
CH = 240
FFP = 16 * CH
WD = 512
TILES = 32
PAIRS = 16
SLOTS = TILES * PAIRS
EPS = 1e-06
LOW = -1e30
SCALE = HD ** (-0.5)
F32 = jnp.float32
BF16 = jnp.bfloat16
MESH = pl.DeviceIdType.MESH

(TBL, RSP, AGQ, PART, AGO, TRA, TGA, SQR, G1, U1, G2, U2, A1, B1, A2, B2, TRB, TGB, N_SEM) = range(19)


def nt(a, b):
    return lax.dot_general(a, b, (((1,), (1,)), ((), ())), preferred_element_type=F32)


def mm(a, b):
    return jnp.dot(a, b, preferred_element_type=F32)


def split(v):
    hi = v.astype(BF16).astype(F32)
    lo = (v - hi).astype(BF16).astype(F32)
    return hi, lo


def kernel(
    x_hbm, gain1, wi_hbm, bias, wo_hbm, gain2, we_hbm, ws_hbm, pc_hbm, tc_hbm, tlen, table,
    x_out, cache_out,
    xb, hb, wi, wo, we, ws, kv, tail,
    tb, tsm, tvm, g01, gm, live01,
    ps, pr, pqkv, qall, qs, us, asend, arecv, oall,
    ys, yr, sqs, sqr, gs, up, g1r, u1r, g1s, u1s, g2r, u2r, ug, acc, tlmask,
    wsem, ssem, rsem,
):
    me = lax.axis_index("kv")
    tp = lax.axis_index("tp")
    y = lax.div(me, 4)
    z = lax.rem(me, 4)

    def kv_at(dy, dz):
        return lax.rem(y + dy, 4) * 4 + lax.rem(z + dz, 4)

    def send(src, dst, ph, to_kv, to_tp):
        pltpu.make_async_remote_copy(
            src_ref=src, dst_ref=dst, send_sem=ssem.at[ph], recv_sem=rsem.at[ph],
            device_id=(to_kv, to_tp), device_id_type=MESH,
        ).start()

    def got(ref, ph):
        pltpu.make_async_copy(ref, ref, rsem.at[ph]).wait()

    def sent(ref, ph):
        pltpu.make_async_copy(ref, ref, ssem.at[ph]).wait()

    def to_all_kv(fn):
        def go(d, c):
            dst = kv_at(lax.div(d, 4), lax.rem(d, 4))
            fn(d, dst)
            return c
        lax.fori_loop(1, 16, go, 0)

    def to_all_tp(fn):
        def go(d, c):
            fn(d, lax.rem(tp + d, 8))
            return c
        lax.fori_loop(1, 8, go, 0)

    loads = [
        pltpu.make_async_copy(x_hbm, xb, wsem.at[0]),
        pltpu.make_async_copy(wi_hbm, wi, wsem.at[1]),
        pltpu.make_async_copy(tc_hbm, tail, wsem.at[2]),
        pltpu.make_async_copy(pc_hbm, kv, wsem.at[3]),
        pltpu.make_async_copy(wo_hbm, wo, wsem.at[4]),
        pltpu.make_async_copy(we_hbm, we.at[:, pl.ds(0, FF)], wsem.at[5]),
        pltpu.make_async_copy(ws_hbm, ws.at[pl.ds(0, FF)], wsem.at[6]),
    ]
    for load in loads:
        load.start()

    barrier = pltpu.get_barrier_semaphore()

    def greet_kv(d, dst):
        pl.semaphore_signal(barrier, inc=1, device_id=(dst, tp), device_id_type=MESH)

    def greet_tp(d, dst):
        pl.semaphore_signal(barrier, inc=1, device_id=(me, dst), device_id_type=MESH)

    to_all_kv(greet_kv)
    to_all_tp(greet_tp)
    pl.semaphore_wait(barrier, 22)

    to_all_kv(lambda d, dst: send(table.at[dst], tb.at[me], TBL, dst, tp))
    tb[me] = table[me]

    for g in range(2):
        we[g, FF:FFP, :] = jnp.zeros((FFP - FF, WD), BF16)
    ws[FF:FFP, :] = jnp.zeros((FFP - FF, WD), BF16)
    cache_out[...] = jnp.zeros_like(cache_out)
    rowmod = lax.rem(lax.broadcasted_iota(jnp.int32, (HEADS * LOC, TAIL), 0), LOC)
    tlm = jnp.zeros((HEADS * LOC, TAIL), jnp.int32)
    for r in range(LOC):
        tlm = jnp.where(rowmod == r, tlen[r], tlm)
    tpos = lax.broadcasted_iota(jnp.int32, (HEADS * LOC, TAIL), 1)
    tlmask[...] = (tpos < tlm).astype(F32)

    def sort_pairs():
        t = tb[...].reshape(ROWS, 128)
        lane = lax.broadcasted_iota(jnp.int32, (ROWS, 128), 1)
        row = lax.broadcasted_iota(jnp.int32, (ROWS, 128), 0)
        valid = lane < BLOCKS
        e0 = jnp.where((t[:, 0:1] == lane) & valid, 1.0, 0.0).astype(F32)
        e1 = jnp.where((t[:, 1:2] == lane) & valid, 1.0, 0.0).astype(F32)
        lower = jnp.where(lane < row, 1.0, 0.0).astype(BF16)
        c0 = mm(lower, e0.astype(BF16))
        c1 = mm(lower, e1.astype(BF16))
        n0 = jnp.sum(e0, axis=0, keepdims=True)
        n1 = jnp.sum(e1, axis=0, keepdims=True)
        n = (n0 + n1).astype(jnp.int32)
        ntile = lax.shift_right_logical(n + (PAIRS - 1), 4).astype(F32)
        upper = jnp.where(row < lane, 1.0, 0.0).astype(BF16)
        nt8 = jnp.broadcast_to(ntile, (8, 128))
        tstart = mm(nt8.astype(BF16), upper)[0:1]
        p0 = jnp.sum(e0 * (PAIRS * tstart + c0), axis=1, keepdims=True)
        p1 = jnp.sum(e1 * (PAIRS * tstart + n0 + c1), axis=1, keepdims=True)
        l0 = jnp.sum(e0, axis=1, keepdims=True)
        l1 = jnp.sum(e1, axis=1, keepdims=True)
        p0 = jnp.where(l0 > 0.5, p0, -1.0).astype(jnp.int32)
        p1 = jnp.where(l1 > 0.5, p1, -1.0).astype(jnp.int32)
        live01[0] = jnp.broadcast_to(l0, (ROWS, 128))
        live01[1] = jnp.broadcast_to(l1, (ROWS, 128))
        slot = lax.broadcasted_iota(jnp.int32, (ROWS, SLOTS), 1)
        h0 = jnp.where(p0 == slot, 1.0, 0.0).astype(F32)
        h1 = jnp.where(p1 == slot, 1.0, 0.0).astype(F32)
        g01[0:ROWS] = h0.astype(BF16)
        g01[ROWS:2 * ROWS] = h1.astype(BF16)
        gm[...] = (h0 + h1).T.astype(BF16)
        tend = tstart + ntile
        ti = lax.broadcasted_iota(jnp.int32, (TILES, 128), 0).astype(F32)
        tl = lax.broadcasted_iota(jnp.int32, (TILES, 128), 1)
        done = jnp.where((tl < BLOCKS) & (tend <= ti), 1.0, 0.0).astype(F32)
        cnt = jnp.minimum(jnp.sum(done, axis=1, keepdims=True), BLOCKS - 1.0)
        tvm[...] = jnp.broadcast_to(cnt, (TILES, 128)).astype(jnp.int32)
        pltpu.sync_copy(tvm, tsm)

    def wait_load(n):
        loads[n].wait()

    def tp_sum(part, ph_r, ph_g, res, dst):
        ys[...] = part.reshape(8, 16, WD).astype(BF16)
        to_all_tp(lambda d, t: send(ys.at[t], yr.at[d - 1], ph_r, me, t))
        total = ys[tp].astype(F32)
        got(yr, ph_r)
        for d in range(7):
            total = total + yr[d].astype(F32)
        dst[tp] = (res[tp].astype(F32) + total.astype(BF16).astype(F32)).astype(BF16)
        sent(yr, ph_r)
        to_all_tp(lambda d, t: send(dst.at[tp], dst.at[tp], ph_g, me, t))
        got(dst.at[pl.ds(0, 7)], ph_g)
        sent(dst.at[pl.ds(0, 7)], ph_g)

    def step(s, carry):
        @pl.when(s == 0)
        def _():
            wait_load(0)
            wait_load(1)

        xf = xb[...].astype(F32).reshape(ROWS, WD)
        sq = jnp.sum(xf * xf, axis=1, keepdims=True)
        a = (xf * gain1[...]).astype(BF16)
        ps[:, :, 0:PW] = mm(a, wi[...]).reshape(16, LOC, PW).astype(BF16)
        hi, lo = split(sq)
        half = lax.broadcasted_iota(jnp.int32, (ROWS, 128), 1) < 64
        ps[:, :, PW:PW + 128] = jnp.where(half, hi, lo).reshape(16, LOC, 128).astype(BF16)
        to_all_kv(lambda d, dst: send(ps.at[dst], pr.at[d - 1], RSP, dst, tp))

        @pl.when(s == 0)
        def _():
            got(tb.at[pl.ds(0, 15)], TBL)
            sent(tb.at[pl.ds(0, 15)], TBL)
            sort_pairs()

        total = ps[me].astype(F32)
        got(pr, RSP)
        for d in range(15):
            total = total + pr[d].astype(F32)
        factor = lax.rsqrt((total[:, PW:PW + 1] + total[:, PW + 64:PW + 65]) / D + EPS)
        proj = (total[:, 0:PW] * factor + bias[...]).astype(BF16)
        pqkv[...] = proj
        cache_out[0, s] = proj[:, QW:QW + HD]
        cache_out[1, s] = proj[:, QW + HD:QW + 2 * HD]
        qall[me] = proj[:, 0:QW]
        sent(pr, RSP)
        to_all_kv(lambda d, dst: send(qall.at[me], qall.at[me], AGQ, dst, tp))

        @pl.when(s == 0)
        def _():
            wait_load(2)

        pf = pqkv[...].astype(F32)
        qh = jnp.concatenate([pf[:, h * HD:(h + 1) * HD] for h in range(HEADS)], axis=0)
        qhb = qh.astype(BF16)
        rm = lax.rem(lax.broadcasted_iota(jnp.int32, (HEADS * LOC, TAIL), 0), LOC)
        sc = jnp.zeros((HEADS * LOC, TAIL), F32)
        for r in range(LOC):
            sc = jnp.where(rm == r, nt(qhb, tail[0, r]), sc)
        sc = sc * SCALE
        tmask = tlmask[...] > 0.5
        sc = jnp.where(tmask, sc, LOW)
        fresh = []
        for t in range(STEPS):
            kf = cache_out[0, t].astype(F32)
            kf = jnp.concatenate([kf] * HEADS, axis=0)
            f = jnp.sum(qh * kf, axis=1, keepdims=True) * SCALE
            fresh.append(jnp.where(t <= s, f, LOW))
        tm = jnp.max(sc, axis=1, keepdims=True)
        for f in fresh:
            tm = jnp.maximum(tm, f)
        e = jnp.where(tmask, jnp.exp(sc - tm), 0.0)
        tl = jnp.sum(e, axis=1, keepdims=True)
        eb = e.astype(BF16)
        tu = jnp.zeros((HEADS * LOC, HD), F32)
        for r in range(LOC):
            tu = tu + mm(jnp.where(rm == r, eb, jnp.zeros_like(eb)), tail[1, r])
        for t in range(STEPS):
            ef = jnp.where(t <= s, jnp.exp(fresh[t] - tm), 0.0)
            tl = tl + ef
            vf = cache_out[1, t].astype(F32)
            tu = tu + ef.astype(BF16).astype(F32) * jnp.concatenate([vf] * HEADS, axis=0)

        got(qall.at[pl.ds(0, 15)], AGQ)
        sent(qall.at[pl.ds(0, 15)], AGQ)
        for h in range(HEADS):
            qa = qall[:, :, h * HD:(h + 1) * HD].astype(F32).reshape(ROWS, HD).astype(BF16)
            qs[h] = mm(gm[...], qa).astype(BF16)

        @pl.when(s == 0)
        def _():
            wait_load(3)

        lane16 = lax.broadcasted_iota(jnp.int32, (PAIRS, 128), 1)

        def tile(t, c):
            b = jnp.minimum(jnp.maximum(tsm[t, 0], 0), BLOCKS - 1)
            at = pl.ds(pl.multiple_of(t * PAIRS, PAIRS), PAIRS)
            q = jnp.concatenate([qs[h, at, :] for h in range(HEADS)], axis=0)
            sc = nt(q, kv[0, b]) * SCALE
            m = jnp.max(sc, axis=1, keepdims=True)
            mh, ml = split(m)
            e = jnp.exp(sc - (mh + ml))
            lh, ll = split(jnp.sum(e, axis=1, keepdims=True))
            u = mm(e.astype(BF16), kv[1, b]).astype(BF16)
            info = jnp.zeros((PAIRS, 128), F32)
            for h in range(HEADS):
                rows = slice(h * PAIRS, (h + 1) * PAIRS)
                us[at, h * HD:(h + 1) * HD] = u[rows]
                info = jnp.where(lane16 == h, mh[rows], info)
                info = jnp.where(lane16 == 8 + h, ml[rows], info)
                info = jnp.where(lane16 == 16 + h, lh[rows], info)
                info = jnp.where(lane16 == 24 + h, ll[rows], info)
            us[at, QW:QW + 128] = info.astype(BF16)
            return c

        lax.fori_loop(0, TILES, tile, 0)

        lane = lax.broadcasted_iota(jnp.int32, (ROWS, 128), 1)
        head = lane < HEADS
        info = mm(g01[...], us[:, QW:QW + 128])
        m01, l01 = [], []
        for c in range(2):
            f = info[c * ROWS:(c + 1) * ROWS]
            m = f + pltpu.roll(f, 120, 1)
            m01.append(jnp.where(head & (live01[c] > 0.5), m, LOW))
            l01.append(pltpu.roll(f, 112, 1) + pltpu.roll(f, 104, 1))
        m = jnp.maximum(m01[0], m01[1])
        w01 = [jnp.where(head & (live01[c] > 0.5), jnp.exp(m01[c] - m), 0.0) for c in range(2)]
        mh, ml = split(jnp.where(head, m, 0.0))
        lh, ll = split(jnp.where(head, w01[0] * l01[0] + w01[1] * l01[1], 0.0))
        packed = mh + pltpu.roll(ml, 8, 1) + pltpu.roll(lh, 16, 1) + pltpu.roll(ll, 24, 1)
        asend[:, :, QW:QW + 128] = packed.reshape(16, LOC, 128).astype(BF16)
        for h in range(HEADS):
            both = mm(g01[...], us[:, h * HD:(h + 1) * HD])
            u = both[0:ROWS] * w01[0][:, h:h + 1] + both[ROWS:] * w01[1][:, h:h + 1]
            asend[:, :, h * HD:(h + 1) * HD] = u.reshape(16, LOC, HD).astype(BF16)
        to_all_kv(lambda d, dst: send(asend.at[dst], arecv.at[d - 1], PART, dst, tp))

        lane8 = lax.broadcasted_iota(jnp.int32, (LOC, 128), 1)
        head8 = lane8 < HEADS
        tmc = jnp.full((LOC, 128), LOW, F32)
        tlc = jnp.zeros((LOC, 128), F32)
        for h in range(HEADS):
            tmc = jnp.where(lane8 == h, tm[h * LOC:(h + 1) * LOC], tmc)
            tlc = jnp.where(lane8 == h, tl[h * LOC:(h + 1) * LOC], tlc)
        arecv[15] = asend[me]
        got(arecv.at[pl.ds(0, 15)], PART)
        sent(arecv.at[pl.ds(0, 15)], PART)
        ms, lsum = [], []
        top = tmc
        for o in range(16):
            f = arecv[o, :, QW:QW + 128].astype(F32)
            m = jnp.where(head8, f + pltpu.roll(f, 120, 1), LOW)
            ms.append(m)
            lsum.append(pltpu.roll(f, 112, 1) + pltpu.roll(f, 104, 1))
            top = jnp.maximum(top, m)
        wt = jnp.exp(tmc - top)
        wo_ = [jnp.exp(m - top) for m in ms]
        den = wt * tlc
        for o in range(16):
            den = den + wo_[o] * lsum[o]
        inv = jnp.where(head8, 1.0 / jnp.where(head8, den, 1.0), 0.0)
        wt = wt * inv
        wo_ = [w * inv for w in wo_]
        for h in range(HEADS):
            o_h = wt[:, h:h + 1] * tu[h * LOC:(h + 1) * LOC]
            for o in range(16):
                o_h = o_h + wo_[o][:, h:h + 1] * arecv[o, :, h * HD:(h + 1) * HD].astype(F32)
            oall[me, :, h * HD:(h + 1) * HD] = o_h.astype(BF16)
        to_all_kv(lambda d, dst: send(oall.at[me], oall.at[me], AGO, dst, tp))

        @pl.when(s == 0)
        def _():
            wait_load(4)

        got(oall.at[pl.ds(0, 15)], AGO)
        sent(oall.at[pl.ds(0, 15)], AGO)
        oa = oall[...].astype(F32).reshape(ROWS, QW).astype(BF16)
        tp_sum(mm(oa, wo[...]), TRA, TGA, xb, hb)

        hf = hb[...].astype(F32).reshape(ROWS, WD)
        sq = jnp.sum(hf * hf, axis=1, keepdims=True)
        sqs[...] = jnp.broadcast_to(sq, (ROWS, 128)).T[0:8]
        to_all_kv(lambda d, dst: send(sqs, sqr.at[d - 1], SQR, dst, tp))
        a2 = (hf * gain2[...]).astype(BF16)

        @pl.when(s == 0)
        def _():
            wait_load(5)

        for k in (2, 1, 3, 0):
            yk = lax.rem(y + k, 4)
            zk = lax.rem(z + k, 4)

            def part(t, c, yk=yk, zk=zk):
                i = yk * 4 + t
                rows = pl.ds(pl.multiple_of(i * CH, 16), CH)
                gs[yk, t] = nt(we[0, rows, :], a2).astype(BF16)
                i = t * 4 + zk
                rows = pl.ds(pl.multiple_of(i * CH, 16), CH)
                up[t, zk] = nt(we[1, rows, :], a2).astype(BF16)
                return c

            lax.fori_loop(0, 4, part, 0)
            if k > 0:
                send(gs.at[yk], g1r.at[k - 1], G1, yk * 4 + z, tp)
                send(up.at[:, zk], u1r.at[k - 1], U1, y * 4 + zk, tp)
        got(g1r, G1)

        def sum1g(t, c):
            v = gs[y, t].astype(F32)
            for d in range(3):
                v = v + g1r[d, t].astype(F32)
            g1s[t] = v.astype(BF16)
            return c

        lax.fori_loop(0, 4, sum1g, 0)
        for k in (2, 1, 3):
            zk = lax.rem(z + k, 4)
            send(g1s.at[zk], g2r.at[k - 1], G2, y * 4 + zk, tp)
        got(u1r, U1)

        def sum1u(t, c):
            v = up[t, z].astype(F32)
            for d in range(3):
                v = v + u1r[d, t].astype(F32)
            u1s[t] = v.astype(BF16)
            return c

        lax.fori_loop(0, 4, sum1u, 0)
        for k in (2, 1, 3):
            yk = lax.rem(y + k, 4)
            send(u1s.at[yk], u2r.at[k - 1], U2, yk * 4 + z, tp)
        got(sqr, SQR)
        sqt = sqs[...]
        for d in range(15):
            sqt = sqt + sqr[d]
        factor = lax.rsqrt(sqt / D + EPS)[0:1]
        got(g2r, G2)
        got(u2r, U2)
        gate = g1s[z].astype(F32)
        upv = u1s[y].astype(F32)
        for d in range(3):
            gate = gate + g2r[d].astype(F32)
            upv = upv + u2r[d].astype(F32)
        gate = gate * factor
        upv = upv * factor
        ug[y, z] = (gate / (1.0 + jnp.exp(-gate)) * upv).astype(BF16)
        sent(sqr, SQR)
        sent(g1r, G1)
        sent(u1r, U1)
        sent(g2r, G2)
        sent(u2r, U2)
        first, second = pl.ds(0, 128), pl.ds(128, CH - 128)
        for k in (2, 1, 3):
            send(ug.at[y, z, first], ug.at[y, z, first], A1, lax.rem(y + k, 4) * 4 + z, tp)
            send(ug.at[y, z, second], ug.at[y, z, second], B1, y * 4 + lax.rem(z + k, 4), tp)
        got(ug.at[0, pl.ds(0, 3), first], A1)
        for k in (2, 1, 3):
            send(ug.at[:, z, first], ug.at[:, z, first], A2, y * 4 + lax.rem(z + k, 4), tp)
        got(ug.at[0, pl.ds(0, 3), second], B1)
        for k in (2, 1, 3):
            send(ug.at[y, :, second], ug.at[y, :, second], B2, lax.rem(y + k, 4) * 4 + z, tp)

        @pl.when(s == 0)
        def _():
            wait_load(6)

        got(ug.at[pl.ds(0, 3), :, first], A2)
        got(ug.at[pl.ds(0, 3), :, second], B2)
        sent(ug.at[0, pl.ds(0, 3), first], A1)
        sent(ug.at[0, pl.ds(0, 3), second], B1)
        sent(ug.at[pl.ds(0, 3), :, first], A2)
        sent(ug.at[pl.ds(0, 3), :, second], B2)
        acc[...] = jnp.zeros_like(acc)

        def down(i, c):
            u = ug[lax.div(i, 4), lax.rem(i, 4)].astype(F32).T.astype(BF16)
            rows = pl.ds(pl.multiple_of(i * CH, 16), CH)
            acc[...] += mm(u, ws[rows, :])
            return c

        lax.fori_loop(0, 16, down, 0)
        tp_sum(acc[...], TRB, TGB, hb, xb)
        return carry

    lax.fori_loop(0, STEPS, step, 0)
    x_out[...] = xb[...]


def layer(x, gain1, wi, bias, wo, gain2, we, ws, pc, tc, tlen, table):
    vmem = pl.BlockSpec(memory_space=pltpu.VMEM)
    smem = pl.BlockSpec(memory_space=pltpu.SMEM)
    hbm = pl.BlockSpec(memory_space=pl.ANY)
    b = lambda *shape: pltpu.VMEM(shape, BF16)
    f = lambda *shape: pltpu.VMEM(shape, F32)
    i = lambda *shape: pltpu.VMEM(shape, jnp.int32)
    return pl.pallas_call(
        kernel,
        out_shape=[
            jax.ShapeDtypeStruct((8, 16, WD), BF16),
            jax.ShapeDtypeStruct((2, STEPS, LOC, HD), BF16),
        ],
        in_specs=[hbm, vmem, hbm, vmem, hbm, vmem, hbm, hbm, hbm, hbm, smem, vmem],
        out_specs=[vmem, vmem],
        scratch_shapes=[
            b(8, 16, WD), b(8, 16, WD),
            b(WD, PW), b(QW, WD), b(2, FFP, WD), b(FFP, WD),
            b(2, BLOCKS, BLOCK, HD), b(2, LOC, TAIL, HD),
            i(16, LOC, 128), pltpu.SMEM((TILES, 128), jnp.int32), i(TILES, 128),
            b(2 * ROWS, SLOTS), b(SLOTS, ROWS), f(2, ROWS, 128),
            b(16, LOC, PW + 128), b(15, LOC, PW + 128), b(LOC, PW),
            b(16, LOC, QW), b(HEADS, SLOTS, HD), b(SLOTS, QW + 128),
            b(16, LOC, QW + 128), b(16, LOC, QW + 128), b(16, LOC, QW),
            b(8, 16, WD), b(7, 16, WD), f(8, 128), f(15, 8, 128),
            b(4, 4, CH, ROWS), b(4, 4, CH, ROWS),
            b(3, 4, CH, ROWS), b(3, 4, CH, ROWS),
            b(4, CH, ROWS), b(4, CH, ROWS), b(3, CH, ROWS), b(3, CH, ROWS),
            b(4, 4, CH, ROWS), f(ROWS, WD), f(HEADS * LOC, TAIL),
            pltpu.SemaphoreType.DMA((7,)),
            pltpu.SemaphoreType.DMA((N_SEM,)),
            pltpu.SemaphoreType.DMA((N_SEM,)),
        ],
        compiler_params=pltpu.CompilerParams(
            collective_id=0, has_side_effects=True, vmem_limit_bytes=56 * 1024 * 1024
        ),
        name="layer",
    )(x, gain1, wi, bias, wo, gain2, we, ws, pc, tc, tlen, table)


def local(
    states, first_gain, input_weight, input_bias, output_weight, second_gain, expand_weight,
    shrink_weight, prompt_cache, tail_cache, tail_length, block_index, block_count,
):
    index = jnp.transpose(block_index[:, 0], (1, 0, 2))
    count = jnp.transpose(block_count[:, 0], (1, 0))
    live = jnp.arange(2, dtype=jnp.int32)[None, None, :] < count[:, :, None]
    table = jnp.where(live, index, BLOCKS)
    table = jnp.pad(table, ((0, 0), (0, 0), (0, 126)), constant_values=BLOCKS)
    x, cache = layer(
        states.reshape(8, 16, WD),
        first_gain.reshape(1, WD),
        input_weight.reshape(WD, PW),
        input_bias.reshape(1, PW).astype(F32),
        output_weight.reshape(QW, WD),
        second_gain.reshape(1, WD),
        jnp.transpose(expand_weight, (1, 2, 0)),
        shrink_weight,
        prompt_cache.reshape(2, BLOCKS, BLOCK, HD),
        tail_cache.reshape(2, LOC, TAIL, HD),
        tail_length,
        table,
    )
    cache = jnp.transpose(cache, (0, 2, 1, 3)).reshape(2, LOC, STEPS, 1, HD)
    return (x.reshape(ROWS, WD), cache)


def solution(mesh):
    return jax.shard_map(
        local,
        mesh=mesh,
        in_specs=(
            P(None, "kv"),
            P("kv"),
            P("kv", "tp", None),
            P("tp", None),
            P("tp", None, "kv"),
            P("kv"),
            P("kv", None, "tp"),
            P("tp", "kv"),
            P(None, "tp", "kv", None, None),
            P(None, "kv", None, "tp", None),
            P("kv"),
            P("kv", "tp", None, None),
            P("kv", "tp", None),
        ),
        out_specs=(P(None, "kv"), P(None, "kv", None, "tp", None)),
        check_vma=False,
    )
```

```python
import functools

import jax
import jax.numpy as jnp
from jax import lax
from jax.experimental import pallas as pl
from jax.experimental.pallas import tpu as pltpu
from jax.sharding import PartitionSpec as P

D = 8192
STEPS = 3
ROWS = 128
LOC = 8
HEADS = 8
HD = 128
QW = HEADS * HD
PW = QW + 2 * HD
BLOCKS = 16
BLOCK = 512
TAIL = 512
FF = 3696
CH = 240
FFP = 16 * CH
WD = 512
TILES = 32
PAIRS = 16
SLOTS = TILES * PAIRS
EPS = 1e-06
LOW = -1e30
SCALE = HD ** (-0.5)
SCALE2 = SCALE * 1.4426950408889634
VW = 2 * HD
F32 = jnp.float32
BF16 = jnp.bfloat16
MESH = pl.DeviceIdType.MESH

(TBL, RSP, AGQ, PART, AGO, TRA, TGA, SQR, TRB, TGB, A1, B1, A2, B2) = range(14)
G1, U1, G2, U2 = (14, 15), (16, 17), (18, 19), (20, 21)
N_SEM = 22
SUBS = ((0, 128), (128, CH - 128))
KV_ORDER = ((2, 2), (1, 2), (2, 1), (3, 2), (2, 3), (0, 2), (2, 0), (1, 1), (3, 3), (1, 3), (3, 1),
            (0, 1), (1, 0), (0, 3), (3, 0))
TP_ORDER = (4, 3, 5, 2, 6, 1, 7)


def nt(a, b):
    return lax.dot_general(a, b, (((1,), (1,)), ((), ())), preferred_element_type=F32)


def tn(a, b):
    return lax.dot_general(a, b, (((0,), (0,)), ((), ())), preferred_element_type=F32)


def mm(a, b):
    return jnp.dot(a, b, preferred_element_type=F32)


def split(v):
    hi = v.astype(BF16).astype(F32)
    lo = (v - hi).astype(BF16).astype(F32)
    return hi, lo


def kernel(
    x_hbm, gain1, wi_hbm, bias, wo_hbm, gain2, we_hbm, ws_hbm, pc_hbm, tc_hbm, tlen, idx, cnt,
    x_out, cache_out,
    xb, hb, wi, wo, wg, wu, ws, keys, vals, tail,
    table, tb, tsm, tvm, g01, gm, live01,
    ps, pr, pqkv, qall, qs, us, asend, arecv, oall,
    ys, yr, sqs, sqr, gs, up, g1r, u1r, g1s, u1s, g2r, u2r, ug, acc, tlmask,
    wsem, ssem, rsem,
):
    me = lax.axis_index("kv")
    tp = lax.axis_index("tp")
    y = lax.div(me, 4)
    z = lax.rem(me, 4)

    def kv_at(dy, dz):
        return lax.rem(y + dy, 4) * 4 + lax.rem(z + dz, 4)

    def send(src, dst, ph, to_kv, to_tp):
        pltpu.make_async_remote_copy(
            src_ref=src, dst_ref=dst, send_sem=ssem.at[ph], recv_sem=rsem.at[ph],
            device_id=(to_kv, to_tp), device_id_type=MESH,
        ).start()

    def got(ref, ph):
        pltpu.make_async_copy(ref, ref, rsem.at[ph]).wait()

    def sent(ref, ph):
        pltpu.make_async_copy(ref, ref, ssem.at[ph]).wait()

    def to_all_kv(fn):
        for dy, dz in KV_ORDER:
            fn(4 * dy + dz, kv_at(dy, dz))

    def to_all_tp(fn):
        for d in TP_ORDER:
            fn(d, lax.rem(tp + d, 8))

    barrier = pltpu.get_barrier_semaphore()
    to_all_kv(lambda d, dst: pl.semaphore_signal(
        barrier, inc=1, device_id=(dst, tp), device_id_type=MESH))
    to_all_tp(lambda d, dst: pl.semaphore_signal(
        barrier, inc=1, device_id=(me, dst), device_id_type=MESH))

    def up_rows(i):
        n = min(CH, FF - i * CH)
        return pltpu.make_async_copy(
            we_hbm.at[1, pl.ds(i * CH, n)], wu.at[i % 4, i // 4, pl.ds(0, n)], wsem.at[8 + i])

    loads = [
        pltpu.make_async_copy(x_hbm, xb, wsem.at[0]),
        pltpu.make_async_copy(wi_hbm, wi, wsem.at[1]),
        pltpu.make_async_copy(tc_hbm, tail, wsem.at[2]),
        pltpu.make_async_copy(pc_hbm.at[0], keys, wsem.at[3]),
        pltpu.make_async_copy(pc_hbm.at[1], vals.at[:, :, pl.ds(0, HD)], wsem.at[4]),
        pltpu.make_async_copy(wo_hbm, wo, wsem.at[5]),
        pltpu.make_async_copy(we_hbm.at[0], wg.at[pl.ds(0, FF)], wsem.at[6]),
        pltpu.make_async_copy(ws_hbm, ws.at[pl.ds(0, FF)], wsem.at[7]),
    ]
    ups = [up_rows(i) for i in range(16)]
    for load in loads + ups:
        load.start()

    table[...] = jnp.zeros_like(table)
    table[0, :, 0:16] = idx[:, 0, :]
    table[1, :, 0:16] = idx[:, 1, :]
    table[2, :, 0:16] = cnt[:, 0, :]
    tb[me] = table[...]

    def project():
        xf = xb[...].astype(F32).reshape(ROWS, WD)
        sq = jnp.sum(xf * xf, axis=1, keepdims=True)
        a = (xf * gain1[...]).astype(BF16)
        ps[:, :, 0:PW] = mm(a, wi[...]).reshape(16, LOC, PW).astype(BF16)
        hi, lo = split(sq)
        half = lax.broadcasted_iota(jnp.int32, (ROWS, 128), 1) < 64
        ps[:, :, PW:PW + 128] = jnp.where(half, hi, lo).reshape(16, LOC, 128).astype(BF16)

    loads[0].wait()
    loads[1].wait()
    project()
    pl.semaphore_wait(barrier, 22)
    to_all_kv(lambda d, dst: send(table, tb.at[me], TBL, dst, tp))

    wg[FF:FFP, :] = jnp.zeros((FFP - FF, WD), BF16)
    wu[3, 3, FF - 15 * CH:CH, :] = jnp.zeros((FFP - FF, WD), BF16)
    vals[:, :, HD:VW] = jnp.ones((BLOCKS, BLOCK, HD), BF16)
    ws[FF:FFP, :] = jnp.zeros((FFP - FF, WD), BF16)
    cache_out[...] = jnp.zeros_like(cache_out)
    rowmod = lax.rem(lax.broadcasted_iota(jnp.int32, (HEADS * LOC, TAIL), 0), LOC)
    tlm = jnp.zeros((HEADS * LOC, TAIL), jnp.int32)
    for r in range(LOC):
        tlm = jnp.where(rowmod == r, tlen[r], tlm)
    tpos = lax.broadcasted_iota(jnp.int32, (HEADS * LOC, TAIL), 1)
    tlmask[...] = (tpos < tlm).astype(F32)

    def sort_pairs():
        lane = lax.broadcasted_iota(jnp.int32, (ROWS, 128), 1)
        row = lax.broadcasted_iota(jnp.int32, (ROWS, 128), 0)
        valid = lane < BLOCKS
        b0, b1, n = [
            jnp.sum(jnp.where(lane == me, tb[:, k].reshape(ROWS, 128).astype(F32), 0.0),
                    axis=1, keepdims=True).astype(jnp.int32) for k in range(3)
        ]
        e0 = jnp.where((b0 == lane) & (n > 0) & valid, 1.0, 0.0).astype(F32)
        e1 = jnp.where((b1 == lane) & (n > 1) & valid, 1.0, 0.0).astype(F32)
        lower = jnp.where(lane < row, 1.0, 0.0).astype(BF16)
        c0 = mm(lower, e0.astype(BF16))
        c1 = mm(lower, e1.astype(BF16))
        n0 = jnp.sum(e0, axis=0, keepdims=True)
        n1 = jnp.sum(e1, axis=0, keepdims=True)
        n = (n0 + n1).astype(jnp.int32)
        ntile = lax.shift_right_logical(n + (PAIRS - 1), 4).astype(F32)
        upper = jnp.where(row < lane, 1.0, 0.0).astype(BF16)
        nt8 = jnp.broadcast_to(ntile, (8, 128))
        tstart = mm(nt8.astype(BF16), upper)[0:1]
        p0 = jnp.sum(e0 * (PAIRS * tstart + c0), axis=1, keepdims=True)
        p1 = jnp.sum(e1 * (PAIRS * tstart + n0 + c1), axis=1, keepdims=True)
        l0 = jnp.sum(e0, axis=1, keepdims=True)
        l1 = jnp.sum(e1, axis=1, keepdims=True)
        p0 = jnp.where(l0 > 0.5, p0, -1.0).astype(jnp.int32)
        p1 = jnp.where(l1 > 0.5, p1, -1.0).astype(jnp.int32)
        live01[0] = jnp.broadcast_to(l0, (ROWS, 128))
        live01[1] = jnp.broadcast_to(l1, (ROWS, 128))
        slot = lax.broadcasted_iota(jnp.int32, (ROWS, SLOTS), 1)
        h0 = jnp.where(p0 == slot, 1.0, 0.0).astype(F32)
        h1 = jnp.where(p1 == slot, 1.0, 0.0).astype(F32)
        g01[0:ROWS] = h0.astype(BF16)
        g01[ROWS:2 * ROWS] = h1.astype(BF16)
        gm[...] = (h0 + h1).T.astype(BF16)
        tend = tstart + ntile
        ti = lax.broadcasted_iota(jnp.int32, (TILES, 128), 0).astype(F32)
        tl = lax.broadcasted_iota(jnp.int32, (TILES, 128), 1)
        done = jnp.where((tl < BLOCKS) & (tend <= ti), 1.0, 0.0).astype(F32)
        cnt = jnp.minimum(jnp.sum(done, axis=1, keepdims=True), BLOCKS - 1.0)
        tvm[...] = jnp.broadcast_to(cnt, (TILES, 128)).astype(jnp.int32)
        pltpu.sync_copy(tvm, tsm)

    def tp_sum(part, ph_r, ph_g, res, dst):
        ys[...] = part.reshape(8, 16, WD).astype(BF16)
        to_all_tp(lambda d, t: send(ys.at[t], yr.at[d - 1], ph_r, me, t))
        total = ys[tp].astype(F32)
        got(yr, ph_r)
        for d in range(7):
            total = total + yr[d].astype(F32)
        dst[tp] = (res[tp].astype(F32) + total.astype(BF16).astype(F32)).astype(BF16)
        sent(yr, ph_r)
        to_all_tp(lambda d, t: send(dst.at[tp], dst.at[tp], ph_g, me, t))
        got(dst.at[pl.ds(0, 7)], ph_g)
        sent(dst.at[pl.ds(0, 7)], ph_g)

    def step(s, carry):
        to_all_kv(lambda d, dst: send(ps.at[dst], pr.at[d - 1], RSP, dst, tp))

        @pl.when(s == 0)
        def _():
            got(tb.at[pl.ds(0, 15)], TBL)
            sent(tb.at[pl.ds(0, 15)], TBL)
            sort_pairs()

        total = ps[me].astype(F32)
        got(pr, RSP)
        for d in range(15):
            total = total + pr[d].astype(F32)
        factor = lax.rsqrt((total[:, PW:PW + 1] + total[:, PW + 64:PW + 65]) / D + EPS)
        proj = (total[:, 0:PW] * factor + bias[...].astype(F32)).astype(BF16)
        pqkv[...] = proj
        cache_out[0, s] = proj[:, QW:QW + HD]
        cache_out[1, s] = proj[:, QW + HD:QW + 2 * HD]
        qall[me] = proj[:, 0:QW]
        sent(pr, RSP)
        to_all_kv(lambda d, dst: send(qall.at[me], qall.at[me], AGQ, dst, tp))

        @pl.when(s == 0)
        def _():
            loads[2].wait()

        pf = pqkv[...].astype(F32)
        qh = jnp.concatenate([pf[:, h * HD:(h + 1) * HD] for h in range(HEADS)], axis=0)
        qhb = qh.astype(BF16)
        rm = lax.rem(lax.broadcasted_iota(jnp.int32, (HEADS * LOC, TAIL), 0), LOC)
        sc = jnp.zeros((HEADS * LOC, TAIL), F32)
        for r in range(LOC):
            sc = jnp.where(rm == r, nt(qhb, tail[0, r]), sc)
        sc = sc * SCALE2
        tmask = tlmask[...] > 0.5
        sc = jnp.where(tmask, sc, LOW)
        fresh = []
        for t in range(STEPS):
            kf = cache_out[0, t].astype(F32)
            kf = jnp.concatenate([kf] * HEADS, axis=0)
            f = jnp.sum(qh * kf, axis=1, keepdims=True) * SCALE2
            fresh.append(jnp.where(t <= s, f, LOW))
        tm = jnp.max(sc, axis=1, keepdims=True)
        for f in fresh:
            tm = jnp.maximum(tm, f)
        e = jnp.where(tmask, jnp.exp2(sc - tm), 0.0)
        tl = jnp.sum(e, axis=1, keepdims=True)
        eb = e.astype(BF16)
        tu = jnp.zeros((HEADS * LOC, HD), F32)
        for r in range(LOC):
            tu = tu + mm(jnp.where(rm == r, eb, jnp.zeros_like(eb)), tail[1, r])
        for t in range(STEPS):
            ef = jnp.where(t <= s, jnp.exp2(fresh[t] - tm), 0.0)
            tl = tl + ef
            vf = cache_out[1, t].astype(F32)
            tu = tu + ef.astype(BF16).astype(F32) * jnp.concatenate([vf] * HEADS, axis=0)

        got(qall.at[pl.ds(0, 15)], AGQ)
        sent(qall.at[pl.ds(0, 15)], AGQ)
        for h in range(0, HEADS, 2):
            qa = qall[:, :, h * HD:(h + 2) * HD].astype(F32).reshape(ROWS, 2 * HD).astype(BF16)
            both = mm(gm[...], qa).astype(BF16)
            qs[h] = both[:, 0:HD]
            qs[h + 1] = both[:, HD:2 * HD]

        @pl.when(s == 0)
        def _():
            loads[3].wait()
            loads[4].wait()

        lane16 = lax.broadcasted_iota(jnp.int32, (PAIRS, 128), 1)

        def tile(t, c):
            b = jnp.minimum(jnp.maximum(tsm[t, 0], 0), BLOCKS - 1)
            at = pl.ds(pl.multiple_of(t * PAIRS, PAIRS), PAIRS)
            q = jnp.concatenate([qs[h, at, :] for h in range(HEADS)], axis=0)
            sc = nt(keys[b], q) * SCALE2
            mh, ml = split(jnp.max(sc, axis=0, keepdims=True))
            m = mh + ml
            e = jnp.exp2(sc - m)
            u = tn(e.astype(BF16), vals[b])
            mt = jnp.broadcast_to(m, (128, 128)).T
            info = jnp.zeros((PAIRS, 128), F32)
            for h in range(HEADS):
                rows = slice(h * PAIRS, (h + 1) * PAIRS)
                us[at, h * HD:(h + 1) * HD] = u[rows, 0:HD].astype(BF16)
                info = jnp.where(lane16 == h, mt[rows], info)
                info = jnp.where(lane16 == 8 + h, u[rows, HD:VW], info)
            hi, lo = split(info)
            us[at, QW:QW + 128] = (hi + pltpu.roll(lo, 16, 1)).astype(BF16)
            return c

        lax.fori_loop(0, TILES, tile, 0, unroll=4)

        lane = lax.broadcasted_iota(jnp.int32, (ROWS, 128), 1)
        head = lane < HEADS
        info = mm(g01[...], us[:, QW:QW + 128])
        m01, l01 = [], []
        for c in range(2):
            f = info[c * ROWS:(c + 1) * ROWS]
            f = f + pltpu.roll(f, 112, 1)
            m01.append(jnp.where(head & (live01[c] > 0.5), f, LOW))
            l01.append(pltpu.roll(f, 120, 1))
        m = jnp.maximum(m01[0], m01[1])
        w01 = [jnp.where(head & (live01[c] > 0.5), jnp.exp2(m01[c] - m), 0.0) for c in range(2)]
        l = jnp.where(head, w01[0] * l01[0] + w01[1] * l01[1], 0.0)
        hi, lo = split(jnp.where(head, m, 0.0) + pltpu.roll(l, 8, 1))
        packed = hi + pltpu.roll(lo, 16, 1)
        asend[:, :, QW:QW + 128] = packed.reshape(16, LOC, 128).astype(BF16)
        for h in range(0, HEADS, 2):
            both = mm(g01[...], us[:, h * HD:(h + 2) * HD])
            for k in range(2):
                cols = slice(k * HD, (k + 1) * HD)
                at = slice((h + k) * HD, (h + k + 1) * HD)
                u = both[0:ROWS, cols] * w01[0][:, h + k:h + k + 1]
                u = u + both[ROWS:, cols] * w01[1][:, h + k:h + k + 1]
                asend[:, :, at] = u.reshape(16, LOC, HD).astype(BF16)
        to_all_kv(lambda d, dst: send(asend.at[dst], arecv.at[d - 1], PART, dst, tp))

        lane8 = lax.broadcasted_iota(jnp.int32, (LOC, 128), 1)
        head8 = lane8 < HEADS
        tmc = jnp.full((LOC, 128), LOW, F32)
        tlc = jnp.zeros((LOC, 128), F32)
        for h in range(HEADS):
            tmc = jnp.where(lane8 == h, tm[h * LOC:(h + 1) * LOC], tmc)
            tlc = jnp.where(lane8 == h, tl[h * LOC:(h + 1) * LOC], tlc)
        arecv[15] = asend[me]
        got(arecv.at[pl.ds(0, 15)], PART)
        sent(arecv.at[pl.ds(0, 15)], PART)
        ms, lsum = [], []
        top = tmc
        for o in range(16):
            f = arecv[o, :, QW:QW + 128].astype(F32)
            f = f + pltpu.roll(f, 112, 1)
            m = jnp.where(head8, f, LOW)
            ms.append(m)
            lsum.append(pltpu.roll(f, 120, 1))
            top = jnp.maximum(top, m)
        wt = jnp.exp2(tmc - top)
        wo_ = [jnp.exp2(m - top) for m in ms]
        den = wt * tlc
        for o in range(16):
            den = den + wo_[o] * lsum[o]
        inv = jnp.where(head8, 1.0 / jnp.where(head8, den, 1.0), 0.0)
        wt = wt * inv
        wo_ = [w * inv for w in wo_]
        for h in range(HEADS):
            o_h = wt[:, h:h + 1] * tu[h * LOC:(h + 1) * LOC]
            for o in range(16):
                o_h = o_h + wo_[o][:, h:h + 1] * arecv[o, :, h * HD:(h + 1) * HD].astype(F32)
            oall[me, :, h * HD:(h + 1) * HD] = o_h.astype(BF16)
        to_all_kv(lambda d, dst: send(oall.at[me], oall.at[me], AGO, dst, tp))

        @pl.when(s == 0)
        def _():
            loads[5].wait()

        got(oall.at[pl.ds(0, 15)], AGO)
        sent(oall.at[pl.ds(0, 15)], AGO)
        oa = oall[...].astype(F32).reshape(ROWS, QW).astype(BF16)
        tp_sum(mm(oa, wo[...]), TRA, TGA, xb, hb)

        hf = hb[...].astype(F32).reshape(ROWS, WD)
        sq = jnp.sum(hf * hf, axis=1, keepdims=True)
        sqs[...] = jnp.broadcast_to(sq, (ROWS, 128)).T[0:8]
        to_all_kv(lambda d, dst: send(sqs, sqr.at[d - 1], SQR, dst, tp))
        a2 = (hf * gain2[...]).astype(BF16)

        @pl.when(s == 0)
        def _():
            loads[6].wait()
            for load in ups:
                load.wait()

        subs = [pl.ds(*sub) for sub in SUBS]
        for k in (2, 1, 3, 0):
            yk = lax.rem(y + k, 4)
            zk = lax.rem(z + k, 4)
            rows = pl.ds(pl.multiple_of(yk * (4 * CH), 16), 4 * CH)
            gs[yk] = nt(wg[rows, :], a2).reshape(4, CH, ROWS).astype(BF16)
            if k > 0:
                send(gs.at[yk, :, subs[0]], g1r.at[k - 1, :, subs[0]], G1[0], yk * 4 + z, tp)
            up[zk] = nt(wu[zk].reshape(4 * CH, WD), a2).reshape(4, CH, ROWS).astype(BF16)
            if k > 0:
                send(up.at[zk, :, subs[0]], u1r.at[k - 1, :, subs[0]], U1[0], y * 4 + zk, tp)
            if k == 3:
                for j in (2, 1, 3):
                    yj = lax.rem(y + j, 4)
                    zj = lax.rem(z + j, 4)
                    send(gs.at[yj, :, subs[1]], g1r.at[j - 1, :, subs[1]], G1[1], yj * 4 + z, tp)
                    send(up.at[zj, :, subs[1]], u1r.at[j - 1, :, subs[1]], U1[1], y * 4 + zj, tp)
        for c, sub in enumerate(subs):
            got(g1r.at[:, :, sub], G1[c])
            v = gs[y, :, sub, :].astype(F32)
            for d in range(3):
                v = v + g1r[d, :, sub, :].astype(F32)
            g1s[:, sub, :] = v.astype(BF16)
            for k in (2, 1, 3):
                zk = lax.rem(z + k, 4)
                send(g1s.at[zk, sub], g2r.at[k - 1, sub], G2[c], y * 4 + zk, tp)
            got(u1r.at[:, :, sub], U1[c])
            v = up[z, :, sub, :].astype(F32)
            for d in range(3):
                v = v + u1r[d, :, sub, :].astype(F32)
            u1s[:, sub, :] = v.astype(BF16)
            for k in (2, 1, 3):
                yk = lax.rem(y + k, 4)
                send(u1s.at[yk, sub], u2r.at[k - 1, sub], U2[c], yk * 4 + z, tp)
        got(sqr, SQR)
        sqt = sqs[...]
        for d in range(15):
            sqt = sqt + sqr[d]
        factor = lax.rsqrt(sqt / D + EPS)[0:1]
        for c, sub in enumerate(subs):
            got(g2r.at[:, sub], G2[c])
            got(u2r.at[:, sub], U2[c])
            gate = g1s[z, sub, :].astype(F32)
            upv = u1s[y, sub, :].astype(F32)
            for d in range(3):
                gate = gate + g2r[d, sub, :].astype(F32)
                upv = upv + u2r[d, sub, :].astype(F32)
            gate = gate * factor
            upv = upv * factor
            ug[y, z, sub, :] = (gate / (1.0 + jnp.exp(-gate)) * upv).astype(BF16)
            for k in (2, 1, 3):
                if c == 0:
                    send(ug.at[y, z, sub], ug.at[y, z, sub], A1, lax.rem(y + k, 4) * 4 + z, tp)
                else:
                    send(ug.at[y, z, sub], ug.at[y, z, sub], B1, y * 4 + lax.rem(z + k, 4), tp)
        got(ug.at[0, pl.ds(0, 3), subs[0]], A1)
        for k in (2, 1, 3):
            zk = lax.rem(z + k, 4)
            send(ug.at[:, z, subs[0]], ug.at[:, z, subs[0]], A2, y * 4 + zk, tp)
        got(ug.at[0, pl.ds(0, 3), subs[1]], B1)
        for k in (2, 1, 3):
            yk = lax.rem(y + k, 4)
            send(ug.at[y, :, subs[1]], ug.at[y, :, subs[1]], B2, yk * 4 + z, tp)
        sent(sqr, SQR)
        for c, sub in enumerate(subs):
            sent(g1r.at[:, :, sub], G1[c])
            sent(u1r.at[:, :, sub], U1[c])
            sent(g2r.at[:, sub], G2[c])
            sent(u2r.at[:, sub], U2[c])

        @pl.when(s == 0)
        def _():
            loads[7].wait()

        for c, sub in enumerate(SUBS):
            got(ug.at[pl.ds(0, 3), :, subs[c]], (A2, B2)[c])
            for half in range(2):
                v = None
                for i in range(8 * half, 8 * half + 8, 2):
                    u = [ug[j // 4, j % 4, sub[0]:sub[0] + sub[1], :] for j in (i, i + 1)]
                    w = [ws[j * CH + sub[0]:j * CH + sub[0] + sub[1], :] for j in (i, i + 1)]
                    p = mm(jnp.concatenate(u, axis=0).T, jnp.concatenate(w, axis=0))
                    v = p if v is None else v + p
                if c == 0 and half == 0:
                    acc[...] = v
                else:
                    acc[...] += v
        sent(ug.at[0, pl.ds(0, 3), subs[0]], A1)
        sent(ug.at[0, pl.ds(0, 3), subs[1]], B1)
        sent(ug.at[pl.ds(0, 3), :, subs[0]], A2)
        sent(ug.at[pl.ds(0, 3), :, subs[1]], B2)
        tp_sum(acc[...], TRB, TGB, hb, xb)

        @pl.when(s < STEPS - 1)
        def _():
            project()

        return carry

    lax.fori_loop(0, STEPS, step, 0)
    x_out[...] = xb[...]


def layer(x, gain1, wi, bias, wo, gain2, we, ws, pc, tc, tlen, idx, cnt):
    vmem = pl.BlockSpec(memory_space=pltpu.VMEM)
    smem = pl.BlockSpec(memory_space=pltpu.SMEM)
    hbm = pl.BlockSpec(memory_space=pl.ANY)
    b = lambda *shape: pltpu.VMEM(shape, BF16)
    f = lambda *shape: pltpu.VMEM(shape, F32)
    i = lambda *shape: pltpu.VMEM(shape, jnp.int32)
    return pl.pallas_call(
        kernel,
        out_shape=[
            jax.ShapeDtypeStruct((8, 16, WD), BF16),
            jax.ShapeDtypeStruct((2, STEPS, LOC, HD), BF16),
        ],
        in_specs=[hbm, vmem, hbm, vmem, hbm, vmem, hbm, hbm, hbm, hbm, smem, vmem, vmem],
        out_specs=[vmem, vmem],
        scratch_shapes=[
            b(8, 16, WD), b(8, 16, WD),
            b(WD, PW), b(QW, WD), b(FFP, WD), b(4, 4, CH, WD), b(FFP, WD),
            b(BLOCKS, BLOCK, HD), b(BLOCKS, BLOCK, VW), b(2, LOC, TAIL, HD),
            i(3, LOC, 128), i(16, 3, LOC, 128), pltpu.SMEM((TILES, 128), jnp.int32), i(TILES, 128),
            b(2 * ROWS, SLOTS), b(SLOTS, ROWS), f(2, ROWS, 128),
            b(16, LOC, PW + 128), b(15, LOC, PW + 128), b(LOC, PW),
            b(16, LOC, QW), b(HEADS, SLOTS, HD), b(SLOTS, QW + 128),
            b(16, LOC, QW + 128), b(16, LOC, QW + 128), b(16, LOC, QW),
            b(8, 16, WD), b(7, 16, WD), f(8, 128), f(15, 8, 128),
            b(4, 4, CH, ROWS), b(4, 4, CH, ROWS),
            b(3, 4, CH, ROWS), b(3, 4, CH, ROWS),
            b(4, CH, ROWS), b(4, CH, ROWS), b(3, CH, ROWS), b(3, CH, ROWS),
            b(4, 4, CH, ROWS), f(ROWS, WD), f(HEADS * LOC, TAIL),
            pltpu.SemaphoreType.DMA((24,)),
            pltpu.SemaphoreType.DMA((N_SEM,)),
            pltpu.SemaphoreType.DMA((N_SEM,)),
        ],
        compiler_params=pltpu.CompilerParams(
            collective_id=0, has_side_effects=True, vmem_limit_bytes=56 * 1024 * 1024
        ),
        name="layer",
    )(x, gain1, wi, bias, wo, gain2, we, ws, pc, tc, tlen, idx, cnt)


def local(
    states, first_gain, input_weight, input_bias, output_weight, second_gain, expand_weight,
    shrink_weight, prompt_cache, tail_cache, tail_length, block_index, block_count,
):
    x, cache = layer(
        states.reshape(8, 16, WD),
        first_gain.reshape(1, WD),
        input_weight.reshape(WD, PW),
        input_bias.reshape(1, PW),
        output_weight.reshape(QW, WD),
        second_gain.reshape(1, WD),
        jnp.transpose(expand_weight, (1, 2, 0)),
        shrink_weight,
        prompt_cache.reshape(2, BLOCKS, BLOCK, HD),
        tail_cache.reshape(2, LOC, TAIL, HD),
        tail_length,
        jnp.transpose(block_index[:, 0], (0, 2, 1)),
        block_count,
    )
    cache = jnp.transpose(cache, (0, 2, 1, 3)).reshape(2, LOC, STEPS, 1, HD)
    return (x.reshape(ROWS, WD), cache)


def solution(mesh):
    return jax.shard_map(
        local,
        mesh=mesh,
        in_specs=(
            P(None, "kv"),
            P("kv"),
            P("kv", "tp", None),
            P("tp", None),
            P("tp", None, "kv"),
            P("kv"),
            P("kv", None, "tp"),
            P("tp", "kv"),
            P(None, "tp", "kv", None, None),
            P(None, "kv", None, "tp", None),
            P("kv"),
            P("kv", "tp", None, None),
            P("kv", "tp", None),
        ),
        out_specs=(P(None, "kv"), P(None, "kv", None, "tp", None)),
        check_vma=False,
    )
```

```python
import functools

import jax
import jax.numpy as jnp
from jax import lax
from jax.experimental import pallas as pl
from jax.experimental.pallas import tpu as pltpu
from jax.sharding import PartitionSpec as P

D = 8192
STEPS = 3
ROWS = 128
LOC = 8
HEADS = 8
HD = 128
QW = HEADS * HD
PW = QW + 2 * HD
BLOCKS = 16
BLOCK = 512
TAIL = 512
FF = 3696
CH = 240
FFP = 16 * CH
WD = 512
TILES = 32
PAIRS = 16
SLOTS = TILES * PAIRS
EPS = 1e-06
LOW = -1e30
SCALE = HD ** (-0.5)
SCALE2 = SCALE * 1.4426950408889634
VW = 2 * HD
F32 = jnp.float32
BF16 = jnp.bfloat16
MESH = pl.DeviceIdType.MESH

(TBL, RSP, AGQ, PART, AGO, TRA, TGA, SQR, TRB, TGB, G2, U2) = range(12)
A1, B1, A2, B2 = (12, 13, 14), (15, 16, 17), (18, 19, 20), (21, 22, 23)
G1, U1 = (24, 25, 26, 27), (28, 29, 30, 31)
N_SEM = 32
SUBS = ((0, 128), (128, CH - 128))
KV_ORDER = ((2, 2), (1, 2), (2, 1), (3, 2), (2, 3), (0, 2), (2, 0), (1, 1), (3, 3), (1, 3), (3, 1),
            (0, 1), (1, 0), (0, 3), (3, 0))
TP_ORDER = (4, 3, 5, 2, 6, 1, 7)


def nt(a, b):
    return lax.dot_general(a, b, (((1,), (1,)), ((), ())), preferred_element_type=F32)


def tn(a, b):
    return lax.dot_general(a, b, (((0,), (0,)), ((), ())), preferred_element_type=F32)


def mm(a, b):
    return jnp.dot(a, b, preferred_element_type=F32)


def split(v):
    hi = v.astype(BF16).astype(F32)
    lo = (v - hi).astype(BF16).astype(F32)
    return hi, lo


def kernel(
    x_hbm, gain1, wi_hbm, bias, wo_hbm, gain2, we_hbm, ws_hbm, pc_hbm, tc_hbm, tlen, idx, cnt,
    x_out, cache_out,
    xb, hb, wi, wo, wg, wu, ws, keys, vals, tail,
    table, tb, tsm, tvm, g01, gm, live01,
    ps, pr, pqkv, qall, qs, us, asend, arecv, oall,
    ys, yr, sqs, sqr, gs, up, g1r, u1r, g1s, u1s, g2r, u2r, ug, acc, tlmask,
    wsem, ssem, rsem,
):
    me = lax.axis_index("kv")
    tp = lax.axis_index("tp")
    y = lax.div(me, 4)
    z = lax.rem(me, 4)

    def kv_at(dy, dz):
        return lax.rem(y + dy, 4) * 4 + lax.rem(z + dz, 4)

    def send(src, dst, ph, to_kv, to_tp):
        pltpu.make_async_remote_copy(
            src_ref=src, dst_ref=dst, send_sem=ssem.at[ph], recv_sem=rsem.at[ph],
            device_id=(to_kv, to_tp), device_id_type=MESH,
        ).start()

    def got(ref, ph):
        pltpu.make_async_copy(ref, ref, rsem.at[ph]).wait()

    def sent(ref, ph):
        pltpu.make_async_copy(ref, ref, ssem.at[ph]).wait()

    def to_all_kv(fn):
        for dy, dz in KV_ORDER:
            fn(4 * dy + dz, kv_at(dy, dz))

    def to_all_tp(fn):
        for d in TP_ORDER:
            fn(d, lax.rem(tp + d, 8))

    barrier = pltpu.get_barrier_semaphore()
    to_all_kv(lambda d, dst: pl.semaphore_signal(
        barrier, inc=1, device_id=(dst, tp), device_id_type=MESH))
    to_all_tp(lambda d, dst: pl.semaphore_signal(
        barrier, inc=1, device_id=(me, dst), device_id_type=MESH))

    def up_rows(i):
        n = min(CH, FF - i * CH)
        return pltpu.make_async_copy(
            we_hbm.at[1, pl.ds(i * CH, n)], wu.at[i % 4, i // 4, pl.ds(0, n)], wsem.at[8 + i])

    loads = [
        pltpu.make_async_copy(x_hbm, xb, wsem.at[0]),
        pltpu.make_async_copy(wi_hbm, wi, wsem.at[1]),
        pltpu.make_async_copy(tc_hbm, tail, wsem.at[2]),
        pltpu.make_async_copy(pc_hbm.at[0], keys, wsem.at[3]),
        pltpu.make_async_copy(pc_hbm.at[1], vals.at[:, :, pl.ds(0, HD)], wsem.at[4]),
        pltpu.make_async_copy(wo_hbm, wo, wsem.at[5]),
        pltpu.make_async_copy(we_hbm.at[0], wg.at[pl.ds(0, FF)], wsem.at[6]),
        pltpu.make_async_copy(ws_hbm, ws.at[pl.ds(0, FF)], wsem.at[7]),
    ]
    ups = [up_rows(i) for i in range(16)]
    for load in loads + ups:
        load.start()

    table[...] = jnp.zeros_like(table)
    table[0, :, 0:16] = idx[:, 0, :]
    table[1, :, 0:16] = idx[:, 1, :]
    table[2, :, 0:16] = cnt[:, 0, :]
    tb[me] = table[...]

    def project():
        xf = xb[...].astype(F32).reshape(ROWS, WD)
        sq = jnp.sum(xf * xf, axis=1, keepdims=True)
        a = (xf * gain1[...]).astype(BF16)
        ps[:, :, 0:PW] = mm(a, wi[...]).reshape(16, LOC, PW).astype(BF16)
        hi, lo = split(sq)
        half = lax.broadcasted_iota(jnp.int32, (ROWS, 128), 1) < 64
        ps[:, :, PW:PW + 128] = jnp.where(half, hi, lo).reshape(16, LOC, 128).astype(BF16)

    loads[0].wait()
    loads[1].wait()
    project()
    pl.semaphore_wait(barrier, 22)
    to_all_kv(lambda d, dst: send(table, tb.at[me], TBL, dst, tp))

    wg[FF:FFP, :] = jnp.zeros((FFP - FF, WD), BF16)
    wu[3, 3, FF - 15 * CH:CH, :] = jnp.zeros((FFP - FF, WD), BF16)
    vals[:, :, HD:VW] = jnp.ones((BLOCKS, BLOCK, HD), BF16)
    ws[FF:FFP, :] = jnp.zeros((FFP - FF, WD), BF16)
    cache_out[...] = jnp.zeros_like(cache_out)
    rowmod = lax.rem(lax.broadcasted_iota(jnp.int32, (HEADS * LOC, TAIL), 0), LOC)
    tlm = jnp.zeros((HEADS * LOC, TAIL), jnp.int32)
    for r in range(LOC):
        tlm = jnp.where(rowmod == r, tlen[r], tlm)
    tpos = lax.broadcasted_iota(jnp.int32, (HEADS * LOC, TAIL), 1)
    tlmask[...] = (tpos < tlm).astype(F32)

    def sort_pairs():
        lane = lax.broadcasted_iota(jnp.int32, (ROWS, 128), 1)
        row = lax.broadcasted_iota(jnp.int32, (ROWS, 128), 0)
        valid = lane < BLOCKS
        b0, b1, n = [
            jnp.sum(jnp.where(lane == me, tb[:, k].reshape(ROWS, 128).astype(F32), 0.0),
                    axis=1, keepdims=True).astype(jnp.int32) for k in range(3)
        ]
        e0 = jnp.where((b0 == lane) & (n > 0) & valid, 1.0, 0.0).astype(F32)
        e1 = jnp.where((b1 == lane) & (n > 1) & valid, 1.0, 0.0).astype(F32)
        lower = jnp.where(lane < row, 1.0, 0.0).astype(BF16)
        c0 = mm(lower, e0.astype(BF16))
        c1 = mm(lower, e1.astype(BF16))
        n0 = jnp.sum(e0, axis=0, keepdims=True)
        n1 = jnp.sum(e1, axis=0, keepdims=True)
        n = (n0 + n1).astype(jnp.int32)
        ntile = lax.shift_right_logical(n + (PAIRS - 1), 4).astype(F32)
        upper = jnp.where(row < lane, 1.0, 0.0).astype(BF16)
        nt8 = jnp.broadcast_to(ntile, (8, 128))
        tstart = mm(nt8.astype(BF16), upper)[0:1]
        p0 = jnp.sum(e0 * (PAIRS * tstart + c0), axis=1, keepdims=True)
        p1 = jnp.sum(e1 * (PAIRS * tstart + n0 + c1), axis=1, keepdims=True)
        l0 = jnp.sum(e0, axis=1, keepdims=True)
        l1 = jnp.sum(e1, axis=1, keepdims=True)
        p0 = jnp.where(l0 > 0.5, p0, -1.0).astype(jnp.int32)
        p1 = jnp.where(l1 > 0.5, p1, -1.0).astype(jnp.int32)
        live01[0] = jnp.broadcast_to(l0, (ROWS, 128))
        live01[1] = jnp.broadcast_to(l1, (ROWS, 128))
        slot = lax.broadcasted_iota(jnp.int32, (ROWS, SLOTS), 1)
        h0 = jnp.where(p0 == slot, 1.0, 0.0).astype(F32)
        h1 = jnp.where(p1 == slot, 1.0, 0.0).astype(F32)
        g01[0:ROWS] = h0.astype(BF16)
        g01[ROWS:2 * ROWS] = h1.astype(BF16)
        gm[...] = (h0 + h1).T.astype(BF16)
        tend = tstart + ntile
        ti = lax.broadcasted_iota(jnp.int32, (TILES, 128), 0).astype(F32)
        tl = lax.broadcasted_iota(jnp.int32, (TILES, 128), 1)
        done = jnp.where((tl < BLOCKS) & (tend <= ti), 1.0, 0.0).astype(F32)
        cnt = jnp.minimum(jnp.sum(done, axis=1, keepdims=True), BLOCKS - 1.0)
        tvm[...] = jnp.broadcast_to(cnt, (TILES, 128)).astype(jnp.int32)
        pltpu.sync_copy(tvm, tsm)

    def tp_sum(part, ph_r, ph_g, res, dst):
        ys[...] = part.reshape(8, 16, WD).astype(BF16)
        to_all_tp(lambda d, t: send(ys.at[t], yr.at[d - 1], ph_r, me, t))
        total = ys[tp].astype(F32)
        got(yr, ph_r)
        for d in range(7):
            total = total + yr[d].astype(F32)
        dst[tp] = (res[tp].astype(F32) + total.astype(BF16).astype(F32)).astype(BF16)
        sent(yr, ph_r)
        to_all_tp(lambda d, t: send(dst.at[tp], dst.at[tp], ph_g, me, t))
        got(dst.at[pl.ds(0, 7)], ph_g)
        sent(dst.at[pl.ds(0, 7)], ph_g)

    def step(s, carry):
        to_all_kv(lambda d, dst: send(ps.at[dst], pr.at[d - 1], RSP, dst, tp))

        total = ps[me].astype(F32)
        got(pr, RSP)
        for d in range(15):
            total = total + pr[d].astype(F32)
        factor = lax.rsqrt((total[:, PW:PW + 1] + total[:, PW + 64:PW + 65]) / D + EPS)
        proj = (total[:, 0:PW] * factor + bias[...].astype(F32)).astype(BF16)
        pqkv[...] = proj
        cache_out[0, s] = proj[:, QW:QW + HD]
        cache_out[1, s] = proj[:, QW + HD:QW + 2 * HD]
        qall[me] = proj[:, 0:QW]
        sent(pr, RSP)
        to_all_kv(lambda d, dst: send(qall.at[me], qall.at[me], AGQ, dst, tp))

        @pl.when(s == 0)
        def _():
            got(tb.at[pl.ds(0, 15)], TBL)
            sent(tb.at[pl.ds(0, 15)], TBL)
            sort_pairs()
            loads[2].wait()

        pf = pqkv[...].astype(F32)
        qh = jnp.concatenate([pf[:, h * HD:(h + 1) * HD] for h in range(HEADS)], axis=0)
        qhb = qh.astype(BF16)
        rm = lax.rem(lax.broadcasted_iota(jnp.int32, (HEADS * LOC, TAIL), 0), LOC)
        sc = jnp.zeros((HEADS * LOC, TAIL), F32)
        for r in range(LOC):
            sc = jnp.where(rm == r, nt(qhb, tail[0, r]), sc)
        sc = sc * SCALE2
        tmask = tlmask[...] > 0.5
        sc = jnp.where(tmask, sc, LOW)
        fresh = []
        for t in range(STEPS):
            kf = cache_out[0, t].astype(F32)
            kf = jnp.concatenate([kf] * HEADS, axis=0)
            f = jnp.sum(qh * kf, axis=1, keepdims=True) * SCALE2
            fresh.append(jnp.where(t <= s, f, LOW))
        tm = jnp.max(sc, axis=1, keepdims=True)
        for f in fresh:
            tm = jnp.maximum(tm, f)
        e = jnp.where(tmask, jnp.exp2(sc - tm), 0.0)
        tl = jnp.sum(e, axis=1, keepdims=True)
        eb = e.astype(BF16)
        tu = jnp.zeros((HEADS * LOC, HD), F32)
        for r in range(LOC):
            tu = tu + mm(jnp.where(rm == r, eb, jnp.zeros_like(eb)), tail[1, r])
        for t in range(STEPS):
            ef = jnp.where(t <= s, jnp.exp2(fresh[t] - tm), 0.0)
            tl = tl + ef
            vf = cache_out[1, t].astype(F32)
            tu = tu + ef.astype(BF16).astype(F32) * jnp.concatenate([vf] * HEADS, axis=0)

        got(qall.at[pl.ds(0, 15)], AGQ)
        sent(qall.at[pl.ds(0, 15)], AGQ)
        for h in range(0, HEADS, 2):
            qa = qall[:, :, h * HD:(h + 2) * HD].astype(F32).reshape(ROWS, 2 * HD).astype(BF16)
            both = mm(gm[...], qa).astype(BF16)
            qs[h] = both[:, 0:HD]
            qs[h + 1] = both[:, HD:2 * HD]

        @pl.when(s == 0)
        def _():
            loads[3].wait()
            loads[4].wait()

        lane16 = lax.broadcasted_iota(jnp.int32, (PAIRS, 128), 1)

        def tile(t, c):
            b = jnp.minimum(jnp.maximum(tsm[t, 0], 0), BLOCKS - 1)
            at = pl.ds(pl.multiple_of(t * PAIRS, PAIRS), PAIRS)
            q = jnp.concatenate([qs[h, at, :] for h in range(HEADS)], axis=0)
            sc = nt(keys[b], q) * SCALE2
            mh, ml = split(jnp.max(sc, axis=0, keepdims=True))
            m = mh + ml
            e = jnp.exp2(sc - m)
            u = tn(e.astype(BF16), vals[b])
            mt = jnp.broadcast_to(m, (128, 128)).T
            info = jnp.zeros((PAIRS, 128), F32)
            for h in range(HEADS):
                rows = slice(h * PAIRS, (h + 1) * PAIRS)
                us[at, h * HD:(h + 1) * HD] = u[rows, 0:HD].astype(BF16)
                info = jnp.where(lane16 == h, mt[rows], info)
                info = jnp.where(lane16 == 8 + h, u[rows, HD:VW], info)
            hi, lo = split(info)
            us[at, QW:QW + 128] = (hi + pltpu.roll(lo, 16, 1)).astype(BF16)
            return c

        lax.fori_loop(0, TILES, tile, 0, unroll=32)

        lane = lax.broadcasted_iota(jnp.int32, (ROWS, 128), 1)
        head = lane < HEADS
        info = mm(g01[...], us[:, QW:QW + 128])
        m01, l01 = [], []
        for c in range(2):
            f = info[c * ROWS:(c + 1) * ROWS]
            f = f + pltpu.roll(f, 112, 1)
            m01.append(jnp.where(head & (live01[c] > 0.5), f, LOW))
            l01.append(pltpu.roll(f, 120, 1))
        m = jnp.maximum(m01[0], m01[1])
        w01 = [jnp.where(head & (live01[c] > 0.5), jnp.exp2(m01[c] - m), 0.0) for c in range(2)]
        l = jnp.where(head, w01[0] * l01[0] + w01[1] * l01[1], 0.0)
        hi, lo = split(jnp.where(head, m, 0.0) + pltpu.roll(l, 8, 1))
        packed = hi + pltpu.roll(lo, 16, 1)
        asend[:, :, QW:QW + 128] = packed.reshape(16, LOC, 128).astype(BF16)
        for h in range(0, HEADS, 2):
            both = mm(g01[...], us[:, h * HD:(h + 2) * HD])
            for k in range(2):
                cols = slice(k * HD, (k + 1) * HD)
                at = slice((h + k) * HD, (h + k + 1) * HD)
                u = both[0:ROWS, cols] * w01[0][:, h + k:h + k + 1]
                u = u + both[ROWS:, cols] * w01[1][:, h + k:h + k + 1]
                asend[:, :, at] = u.reshape(16, LOC, HD).astype(BF16)
        to_all_kv(lambda d, dst: send(asend.at[dst], arecv.at[d - 1], PART, dst, tp))

        lane8 = lax.broadcasted_iota(jnp.int32, (LOC, 128), 1)
        head8 = lane8 < HEADS
        tmc = jnp.full((LOC, 128), LOW, F32)
        tlc = jnp.zeros((LOC, 128), F32)
        for h in range(HEADS):
            tmc = jnp.where(lane8 == h, tm[h * LOC:(h + 1) * LOC], tmc)
            tlc = jnp.where(lane8 == h, tl[h * LOC:(h + 1) * LOC], tlc)
        arecv[15] = asend[me]
        got(arecv.at[pl.ds(0, 15)], PART)
        sent(arecv.at[pl.ds(0, 15)], PART)
        ms, lsum = [], []
        top = tmc
        for o in range(16):
            f = arecv[o, :, QW:QW + 128].astype(F32)
            f = f + pltpu.roll(f, 112, 1)
            m = jnp.where(head8, f, LOW)
            ms.append(m)
            lsum.append(pltpu.roll(f, 120, 1))
            top = jnp.maximum(top, m)
        wt = jnp.exp2(tmc - top)
        wo_ = [jnp.exp2(m - top) for m in ms]
        den = wt * tlc
        for o in range(16):
            den = den + wo_[o] * lsum[o]
        inv = jnp.where(head8, 1.0 / jnp.where(head8, den, 1.0), 0.0)
        wt = wt * inv
        wo_ = [w * inv for w in wo_]
        for h in range(HEADS):
            o_h = wt[:, h:h + 1] * tu[h * LOC:(h + 1) * LOC]
            for o in range(16):
                o_h = o_h + wo_[o][:, h:h + 1] * arecv[o, :, h * HD:(h + 1) * HD].astype(F32)
            oall[me, :, h * HD:(h + 1) * HD] = o_h.astype(BF16)
        to_all_kv(lambda d, dst: send(oall.at[me], oall.at[me], AGO, dst, tp))

        @pl.when(s == 0)
        def _():
            loads[5].wait()

        got(oall.at[pl.ds(0, 15)], AGO)
        sent(oall.at[pl.ds(0, 15)], AGO)
        oa = oall[...].astype(F32).reshape(ROWS, QW).astype(BF16)
        tp_sum(mm(oa, wo[...]), TRA, TGA, xb, hb)

        hf = hb[...].astype(F32).reshape(ROWS, WD)
        sq = jnp.sum(hf * hf, axis=1, keepdims=True)
        sqs[...] = jnp.broadcast_to(sq, (ROWS, 128)).T[0:8]
        a2 = (hf * gain2[...]).astype(BF16)

        @pl.when(s == 0)
        def _():
            loads[6].wait()
            for load in ups:
                load.wait()

        for off in (2, 1, 3, 0):
            yk = lax.rem(y + off, 4)
            zk = lax.rem(z + off, 4)
            rows = pl.ds(pl.multiple_of(yk * (4 * CH), 16), 4 * CH)
            gs[yk] = nt(wg[rows, :], a2).reshape(4, CH, ROWS).astype(BF16)
            for k in (2, 1, 3):
                zt = lax.rem(z + k, 4)
                send(gs.at[yk, zt], g1r.at[off, k - 1], G1[off], y * 4 + zt, tp)
            up[zk] = nt(wu[zk].reshape(4 * CH, WD), a2).reshape(4, CH, ROWS).astype(BF16)
            for k in (2, 1, 3):
                yt = lax.rem(y + k, 4)
                send(up.at[zk, yt], u1r.at[off, k - 1], U1[off], yt * 4 + z, tp)
            if off == 2:
                to_all_kv(lambda d, dst: send(sqs, sqr.at[d - 1], SQR, dst, tp))
        for off in (2, 1, 3, 0):
            yk = lax.rem(y + off, 4)
            zk = lax.rem(z + off, 4)
            got(g1r.at[off], G1[off])
            gate = gs[yk, z].astype(F32)
            for d in range(3):
                gate = gate + g1r[off, d].astype(F32)
            if off > 0:
                g1s[off - 1] = gate.astype(BF16)
                send(g1s.at[off - 1], g2r.at[off - 1], G2, yk * 4 + z, tp)
            got(u1r.at[off], U1[off])
            upv = up[zk, y].astype(F32)
            for d in range(3):
                upv = upv + u1r[off, d].astype(F32)
            if off > 0:
                u1s[off - 1] = upv.astype(BF16)
                send(u1s.at[off - 1], u2r.at[off - 1], U2, y * 4 + zk, tp)
        got(sqr, SQR)
        sqt = sqs[...]
        for d in range(15):
            sqt = sqt + sqr[d]
        factor = lax.rsqrt(sqt / D + EPS)[0:1]
        got(g2r, G2)
        got(u2r, U2)
        for d in range(3):
            gate = gate + g2r[d].astype(F32)
            upv = upv + u2r[d].astype(F32)
        gate = gate * factor
        upv = upv * factor
        ug[y, z] = (gate / (1.0 + jnp.exp(-gate)) * upv).astype(BF16)

        subs = [pl.ds(*sub) for sub in SUBS]
        first, second = ug.at[y, z, subs[0]], ug.at[y, z, subs[1]]
        for k in (2, 1, 3):
            send(first, first, A1[k - 1], lax.rem(y + k, 4) * 4 + z, tp)
            send(second, second, B1[k - 1], y * 4 + lax.rem(z + k, 4), tp)
        for k in (2, 1, 3):
            send(first, first, A2[k - 1], y * 4 + lax.rem(z + k, 4), tp)
            send(second, second, B2[k - 1], lax.rem(y + k, 4) * 4 + z, tp)
        for d in (1, 3, 2):
            slab = ug.at[lax.rem(y + 4 - d, 4), z, subs[0]]
            got(slab, A1[d - 1])
            for k in (2, 1, 3):
                send(slab, slab, A2[k - 1], y * 4 + lax.rem(z + k, 4), tp)
            slab = ug.at[y, lax.rem(z + 4 - d, 4), subs[1]]
            got(slab, B1[d - 1])
            for k in (2, 1, 3):
                send(slab, slab, B2[k - 1], lax.rem(y + k, 4) * 4 + z, tp)
        sent(sqr, SQR)
        for off in range(4):
            sent(g1r.at[off], G1[off])
            sent(u1r.at[off], U1[off])
        sent(g2r, G2)
        sent(u2r, U2)

        @pl.when(s == 0)
        def _():
            loads[7].wait()

        def down(c, at):
            lo, n = SUBS[c]
            spots = [(t, at) if c == 0 else (at, t) for t in range(4)]
            u = [ug[i, j, lo:lo + n, :] for i, j in spots]
            w = [ws[pl.ds(pl.multiple_of((i * 4 + j) * CH + lo, 16), n), :] for i, j in spots]
            return mm(jnp.concatenate(u, axis=0).T, jnp.concatenate(w, axis=0))

        acc[...] = down(0, z)
        acc[...] += down(1, y)
        for d in (1, 3, 2):
            got(ug.at[:, 0, subs[0]], A2[d - 1])
            acc[...] += down(0, lax.rem(z + 4 - d, 4))
            got(ug.at[0, :, subs[1]], B2[d - 1])
            acc[...] += down(1, lax.rem(y + 4 - d, 4))
        for d in range(3):
            sent(first, A1[d])
            sent(second, B1[d])
            sent(ug.at[:, 0, subs[0]], A2[d])
            sent(ug.at[0, :, subs[1]], B2[d])
        tp_sum(acc[...], TRB, TGB, hb, xb)

        @pl.when(s < STEPS - 1)
        def _():
            project()

        return carry

    lax.fori_loop(0, STEPS, step, 0)
    x_out[...] = xb[...]


def layer(x, gain1, wi, bias, wo, gain2, we, ws, pc, tc, tlen, idx, cnt):
    vmem = pl.BlockSpec(memory_space=pltpu.VMEM)
    smem = pl.BlockSpec(memory_space=pltpu.SMEM)
    hbm = pl.BlockSpec(memory_space=pl.ANY)
    b = lambda *shape: pltpu.VMEM(shape, BF16)
    f = lambda *shape: pltpu.VMEM(shape, F32)
    i = lambda *shape: pltpu.VMEM(shape, jnp.int32)
    return pl.pallas_call(
        kernel,
        out_shape=[
            jax.ShapeDtypeStruct((8, 16, WD), BF16),
            jax.ShapeDtypeStruct((2, STEPS, LOC, HD), BF16),
        ],
        in_specs=[hbm, vmem, hbm, vmem, hbm, vmem, hbm, hbm, hbm, hbm, smem, vmem, vmem],
        out_specs=[vmem, vmem],
        scratch_shapes=[
            b(8, 16, WD), b(8, 16, WD),
            b(WD, PW), b(QW, WD), b(FFP, WD), b(4, 4, CH, WD), b(FFP, WD),
            b(BLOCKS, BLOCK, HD), b(BLOCKS, BLOCK, VW), b(2, LOC, TAIL, HD),
            i(3, LOC, 128), i(16, 3, LOC, 128), pltpu.SMEM((TILES, 128), jnp.int32), i(TILES, 128),
            b(2 * ROWS, SLOTS), b(SLOTS, ROWS), f(2, ROWS, 128),
            b(16, LOC, PW + 128), b(15, LOC, PW + 128), b(LOC, PW),
            b(16, LOC, QW), b(HEADS, SLOTS, HD), b(SLOTS, QW + 128),
            b(16, LOC, QW + 128), b(16, LOC, QW + 128), b(16, LOC, QW),
            b(8, 16, WD), b(7, 16, WD), f(8, 128), f(15, 8, 128),
            b(4, 4, CH, ROWS), b(4, 4, CH, ROWS),
            b(4, 3, CH, ROWS), b(4, 3, CH, ROWS),
            b(3, CH, ROWS), b(3, CH, ROWS), b(3, CH, ROWS), b(3, CH, ROWS),
            b(4, 4, CH, ROWS), f(ROWS, WD), f(HEADS * LOC, TAIL),
            pltpu.SemaphoreType.DMA((24,)),
            pltpu.SemaphoreType.DMA((N_SEM,)),
            pltpu.SemaphoreType.DMA((N_SEM,)),
        ],
        compiler_params=pltpu.CompilerParams(
            collective_id=0, has_side_effects=True, vmem_limit_bytes=56 * 1024 * 1024
        ),
        name="layer",
    )(x, gain1, wi, bias, wo, gain2, we, ws, pc, tc, tlen, idx, cnt)


def copies(x, cache, x_out, cache_out):
    x_out[...] = x[...]
    cache_out[...] = cache[...]


def write(x, cache):
    vmem = pl.BlockSpec(memory_space=pltpu.VMEM)
    return pl.pallas_call(
        copies,
        out_shape=[jax.ShapeDtypeStruct(x.shape, x.dtype), jax.ShapeDtypeStruct(cache.shape, cache.dtype)],
        in_specs=[vmem, vmem],
        out_specs=[vmem, vmem],
        name="write",
    )(x, cache)


def local(
    states, first_gain, input_weight, input_bias, output_weight, second_gain, expand_weight,
    shrink_weight, prompt_cache, tail_cache, tail_length, block_index, block_count,
):
    x, cache = layer(
        states.reshape(8, 16, WD),
        first_gain.reshape(1, WD),
        input_weight.reshape(WD, PW),
        input_bias.reshape(1, PW),
        output_weight.reshape(QW, WD),
        second_gain.reshape(1, WD),
        jnp.transpose(expand_weight, (1, 2, 0)),
        shrink_weight,
        prompt_cache.reshape(2, BLOCKS, BLOCK, HD),
        tail_cache.reshape(2, LOC, TAIL, HD),
        tail_length,
        jnp.transpose(block_index[:, 0], (0, 2, 1)),
        block_count,
    )
    x, cache = write(x, cache)
    cache = jnp.transpose(cache, (0, 2, 1, 3)).reshape(2, LOC, STEPS, 1, HD)
    return (x.reshape(ROWS, WD), cache)


def solution(mesh):
    return jax.shard_map(
        local,
        mesh=mesh,
        in_specs=(
            P(None, "kv"),
            P("kv"),
            P("kv", "tp", None),
            P("tp", None),
            P("tp", None, "kv"),
            P("kv"),
            P("kv", None, "tp"),
            P("tp", "kv"),
            P(None, "tp", "kv", None, None),
            P(None, "kv", None, "tp", None),
            P("kv"),
            P("kv", "tp", None, None),
            P("kv", "tp", None),
        ),
        out_specs=(P(None, "kv"), P(None, "kv", None, "tp", None)),
        check_vma=False,
    )
```

```python
import functools

import jax
import jax.numpy as jnp
from jax import lax
from jax.experimental import pallas as pl
from jax.experimental.pallas import tpu as pltpu
from jax.sharding import PartitionSpec as P

D = 8192
STEPS = 3
ROWS = 128
LOC = 8
HEADS = 8
HD = 128
QW = HEADS * HD
PW = QW + 2 * HD
BLOCKS = 16
BLOCK = 512
TAIL = 512
FF = 3696
CH = 240
FFP = 16 * CH
WD = 512
TILES = 32
PAIRS = 16
SLOTS = TILES * PAIRS
EPS = 1e-06
LOW = -1e30
SCALE = HD ** (-0.5)
SCALE2 = SCALE * 1.4426950408889634
VW = 2 * HD
F32 = jnp.float32
BF16 = jnp.bfloat16
MESH = pl.DeviceIdType.MESH

(TBL, RSP, AGQ, PART, AGO, TRA, TGA, SQR, TRB, TGB, G2, U2) = range(12)
A1, B1, A2, B2 = (12, 13, 14), (15, 16, 17), (18, 19, 20), (21, 22, 23)
G1, U1 = (24, 25, 26, 27), (28, 29, 30, 31)
RG, RU = (32, 33, 34), (35, 36, 37)
TA, TB = (TRA, TGA, 38), (TRB, TGB, 39)
N_SEM = 40
SUBS = ((0, 128), (128, CH - 128))
KV_ORDER = ((2, 2), (1, 2), (2, 1), (3, 2), (2, 3), (0, 2), (2, 0), (1, 1), (3, 3), (1, 3), (3, 1),
            (0, 1), (1, 0), (0, 3), (3, 0))
TP_ORDER = (4, 3, 5, 2, 6, 1, 7)


def nt(a, b):
    return lax.dot_general(a, b, (((1,), (1,)), ((), ())), preferred_element_type=F32)


def tn(a, b):
    return lax.dot_general(a, b, (((0,), (0,)), ((), ())), preferred_element_type=F32)


def mm(a, b):
    return jnp.dot(a, b, preferred_element_type=F32)


def split(v):
    hi = v.astype(BF16).astype(F32)
    lo = (v - hi).astype(BF16).astype(F32)
    return hi, lo


def kernel(
    x_hbm, gain1, wi_hbm, bias, wo_hbm, gain2, we_hbm, ws_hbm, pc_hbm, tc_hbm, tlen, idx, cnt,
    x_out, cache_out,
    xb, hb, wi, wo, wg, wu, ws, keys, vals, tail,
    table, tb, tsm, tvm, g01, gm, live01,
    ps, pr, pqkv, qall, qs, us, asend, arecv, oall,
    ys, sib, xra, xrb, sqs, sqr, gs, up, rlg, rlu, crg, cru, g1r, u1r, g1s, u1s, g2r, u2r, ug, acc, tlmask,
    wsem, ssem, rsem,
):
    me = lax.axis_index("kv")
    tp = lax.axis_index("tp")
    y = lax.div(me, 4)
    z = lax.rem(me, 4)

    def kv_at(dy, dz):
        return lax.rem(y + dy, 4) * 4 + lax.rem(z + dz, 4)

    def send(src, dst, ph, to_kv, to_tp):
        pltpu.make_async_remote_copy(
            src_ref=src, dst_ref=dst, send_sem=ssem.at[ph], recv_sem=rsem.at[ph],
            device_id=(to_kv, to_tp), device_id_type=MESH,
        ).start()

    def got(ref, ph):
        pltpu.make_async_copy(ref, ref, rsem.at[ph]).wait()

    def sent(ref, ph):
        pltpu.make_async_copy(ref, ref, ssem.at[ph]).wait()

    def to_all_kv(fn):
        for dy, dz in KV_ORDER:
            fn(4 * dy + dz, kv_at(dy, dz))

    def to_all_tp(fn):
        for d in TP_ORDER:
            fn(d, lax.rem(tp + d, 8))

    barrier = pltpu.get_barrier_semaphore()
    to_all_kv(lambda d, dst: pl.semaphore_signal(
        barrier, inc=1, device_id=(dst, tp), device_id_type=MESH))
    to_all_tp(lambda d, dst: pl.semaphore_signal(
        barrier, inc=1, device_id=(me, dst), device_id_type=MESH))

    def up_rows(i):
        n = min(CH, FF - i * CH)
        return pltpu.make_async_copy(
            we_hbm.at[1, pl.ds(i * CH, n)], wu.at[i % 4, i // 4, pl.ds(0, n)], wsem.at[8 + i])

    loads = [
        pltpu.make_async_copy(x_hbm, xb, wsem.at[0]),
        pltpu.make_async_copy(wi_hbm, wi, wsem.at[1]),
        pltpu.make_async_copy(tc_hbm, tail, wsem.at[2]),
        pltpu.make_async_copy(pc_hbm.at[0], keys, wsem.at[3]),
        pltpu.make_async_copy(pc_hbm.at[1], vals.at[:, :, pl.ds(0, HD)], wsem.at[4]),
        pltpu.make_async_copy(wo_hbm, wo, wsem.at[5]),
        pltpu.make_async_copy(we_hbm.at[0], wg.at[pl.ds(0, FF)], wsem.at[6]),
        pltpu.make_async_copy(ws_hbm, ws.at[pl.ds(0, FF)], wsem.at[7]),
    ]
    ups = [up_rows(i) for i in range(16)]
    for load in loads + ups:
        load.start()

    table[...] = jnp.zeros_like(table)
    table[0, :, 0:16] = idx[:, 0, :]
    table[1, :, 0:16] = idx[:, 1, :]
    table[2, :, 0:16] = cnt[:, 0, :]
    tb[me] = table[...]

    def project():
        xf = xb[...].astype(F32).reshape(ROWS, WD)
        sq = jnp.sum(xf * xf, axis=1, keepdims=True)
        a = (xf * gain1[...]).astype(BF16)
        ps[:, :, 0:PW] = mm(a, wi[...]).reshape(16, LOC, PW).astype(BF16)
        hi, lo = split(sq)
        half = lax.broadcasted_iota(jnp.int32, (ROWS, 128), 1) < 64
        ps[:, :, PW:PW + 128] = jnp.where(half, hi, lo).reshape(16, LOC, 128).astype(BF16)

    wg[FF:FFP, :] = jnp.zeros((FFP - FF, WD), BF16)
    wu[3, 3, FF - 15 * CH:CH, :] = jnp.zeros((FFP - FF, WD), BF16)
    vals[:, :, HD:VW] = jnp.ones((BLOCKS, BLOCK, HD), BF16)
    ws[FF:FFP, :] = jnp.zeros((FFP - FF, WD), BF16)
    cache_out[...] = jnp.zeros_like(cache_out)
    rowmod = lax.rem(lax.broadcasted_iota(jnp.int32, (HEADS * LOC, TAIL), 0), LOC)
    tlm = jnp.zeros((HEADS * LOC, TAIL), jnp.int32)
    for r in range(LOC):
        tlm = jnp.where(rowmod == r, tlen[r], tlm)
    tpos = lax.broadcasted_iota(jnp.int32, (HEADS * LOC, TAIL), 1)
    tlmask[...] = (tpos < tlm).astype(F32)

    loads[0].wait()
    loads[1].wait()
    project()
    pl.semaphore_wait(barrier, 22)

    def sort_pairs():
        lane = lax.broadcasted_iota(jnp.int32, (ROWS, 128), 1)
        row = lax.broadcasted_iota(jnp.int32, (ROWS, 128), 0)
        valid = lane < BLOCKS
        b0, b1, n = [
            jnp.sum(jnp.where(lane == me, tb[:, k].reshape(ROWS, 128).astype(F32), 0.0),
                    axis=1, keepdims=True).astype(jnp.int32) for k in range(3)
        ]
        e0 = jnp.where((b0 == lane) & (n > 0) & valid, 1.0, 0.0).astype(F32)
        e1 = jnp.where((b1 == lane) & (n > 1) & valid, 1.0, 0.0).astype(F32)
        lower = jnp.where(lane < row, 1.0, 0.0).astype(BF16)
        c0 = mm(lower, e0.astype(BF16))
        c1 = mm(lower, e1.astype(BF16))
        n0 = jnp.sum(e0, axis=0, keepdims=True)
        n1 = jnp.sum(e1, axis=0, keepdims=True)
        n = (n0 + n1).astype(jnp.int32)
        ntile = lax.shift_right_logical(n + (PAIRS - 1), 4).astype(F32)
        upper = jnp.where(row < lane, 1.0, 0.0).astype(BF16)
        nt8 = jnp.broadcast_to(ntile, (8, 128))
        tstart = mm(nt8.astype(BF16), upper)[0:1]
        p0 = jnp.sum(e0 * (PAIRS * tstart + c0), axis=1, keepdims=True)
        p1 = jnp.sum(e1 * (PAIRS * tstart + n0 + c1), axis=1, keepdims=True)
        l0 = jnp.sum(e0, axis=1, keepdims=True)
        l1 = jnp.sum(e1, axis=1, keepdims=True)
        p0 = jnp.where(l0 > 0.5, p0, -1.0).astype(jnp.int32)
        p1 = jnp.where(l1 > 0.5, p1, -1.0).astype(jnp.int32)
        live01[0] = jnp.broadcast_to(l0, (ROWS, 128))
        live01[1] = jnp.broadcast_to(l1, (ROWS, 128))
        slot = lax.broadcasted_iota(jnp.int32, (ROWS, SLOTS), 1)
        h0 = jnp.where(p0 == slot, 1.0, 0.0).astype(F32)
        h1 = jnp.where(p1 == slot, 1.0, 0.0).astype(F32)
        g01[0:ROWS] = h0.astype(BF16)
        g01[ROWS:2 * ROWS] = h1.astype(BF16)
        gm[...] = (h0 + h1).T.astype(BF16)
        tend = tstart + ntile
        ti = lax.broadcasted_iota(jnp.int32, (TILES, 128), 0).astype(F32)
        tl = lax.broadcasted_iota(jnp.int32, (TILES, 128), 1)
        done = jnp.where((tl < BLOCKS) & (tend <= ti), 1.0, 0.0).astype(F32)
        cnt = jnp.minimum(jnp.sum(done, axis=1, keepdims=True), BLOCKS - 1.0)
        tvm[...] = jnp.broadcast_to(cnt, (TILES, 128)).astype(jnp.int32)
        pltpu.sync_copy(tvm, tsm)

    core = lax.rem(tp, 2)
    chip = lax.div(tp, 2)
    sibling = tp + 1 - 2 * core

    def tp_sum(part, ph, xr, res, dst):
        ys[...] = part.reshape(2, 64, WD).astype(BF16)
        send(ys.at[1 - core], sib, ph[0], me, sibling)
        own = ys[core].astype(F32)
        got(sib, ph[0])
        xr[chip] = (own + sib[...].astype(F32)).astype(BF16)
        for d in (2, 1, 3):
            send(xr.at[chip], xr.at[chip], ph[1], me, lax.rem(tp + 2 * d, 8))
        sent(sib, ph[0])
        got(xr.at[pl.ds(0, 3)], ph[1])
        total = xr[0].astype(F32)
        for d in range(1, 4):
            total = total + xr[d].astype(F32)
        dst[core] = (res[core].astype(F32) + total.astype(BF16).astype(F32)).astype(BF16)
        send(dst.at[core], dst.at[core], ph[2], me, sibling)
        sent(xr.at[pl.ds(0, 3)], ph[1])
        got(dst.at[0], ph[2])

    def step(s, carry):
        to_all_kv(lambda d, dst: send(ps.at[dst], pr.at[d - 1], RSP, dst, tp))

        @pl.when(s == 0)
        def _():
            to_all_kv(lambda d, dst: send(table, tb.at[me], TBL, dst, tp))

        @pl.when(s > 0)
        def _():
            sent(xb.at[0], TB[2])


        total = ps[me].astype(F32)
        got(pr, RSP)
        for d in range(15):
            total = total + pr[d].astype(F32)
        factor = lax.rsqrt((total[:, PW:PW + 1] + total[:, PW + 64:PW + 65]) / D + EPS)
        proj = (total[:, 0:PW] * factor + bias[...].astype(F32)).astype(BF16)
        pqkv[...] = proj
        cache_out[0, s] = proj[:, QW:QW + HD]
        cache_out[1, s] = proj[:, QW + HD:QW + 2 * HD]
        qall[me] = proj[:, 0:QW]
        to_all_kv(lambda d, dst: send(qall.at[me], qall.at[me], AGQ, dst, tp))
        sent(pr, RSP)

        @pl.when(s == 0)
        def _():
            got(tb.at[pl.ds(0, 15)], TBL)
            sent(tb.at[pl.ds(0, 15)], TBL)
            sort_pairs()
            loads[2].wait()

        pf = pqkv[...].astype(F32)
        qh = jnp.concatenate([pf[:, h * HD:(h + 1) * HD] for h in range(HEADS)], axis=0)
        qhb = qh.astype(BF16)
        rm = lax.rem(lax.broadcasted_iota(jnp.int32, (HEADS * LOC, TAIL), 0), LOC)
        sc = jnp.zeros((HEADS * LOC, TAIL), F32)
        for r in range(LOC):
            sc = jnp.where(rm == r, nt(qhb, tail[0, r]), sc)
        sc = sc * SCALE2
        tmask = tlmask[...] > 0.5
        sc = jnp.where(tmask, sc, LOW)
        fresh = []
        for t in range(STEPS):
            kf = cache_out[0, t].astype(F32)
            kf = jnp.concatenate([kf] * HEADS, axis=0)
            f = jnp.sum(qh * kf, axis=1, keepdims=True) * SCALE2
            fresh.append(jnp.where(t <= s, f, LOW))
        tm = jnp.max(sc, axis=1, keepdims=True)
        for f in fresh:
            tm = jnp.maximum(tm, f)
        e = jnp.where(tmask, jnp.exp2(sc - tm), 0.0)
        tl = jnp.sum(e, axis=1, keepdims=True)
        eb = e.astype(BF16)
        tu = jnp.zeros((HEADS * LOC, HD), F32)
        for r in range(LOC):
            tu = tu + mm(jnp.where(rm == r, eb, jnp.zeros_like(eb)), tail[1, r])
        for t in range(STEPS):
            ef = jnp.where(t <= s, jnp.exp2(fresh[t] - tm), 0.0)
            tl = tl + ef
            vf = cache_out[1, t].astype(F32)
            tu = tu + ef.astype(BF16).astype(F32) * jnp.concatenate([vf] * HEADS, axis=0)

        got(qall.at[pl.ds(0, 15)], AGQ)
        for h in range(0, HEADS, 2):
            qa = qall[:, :, h * HD:(h + 2) * HD].astype(F32).reshape(ROWS, 2 * HD).astype(BF16)
            both = mm(gm[...], qa).astype(BF16)
            qs[h] = both[:, 0:HD]
            qs[h + 1] = both[:, HD:2 * HD]

        @pl.when(s == 0)
        def _():
            loads[3].wait()
            loads[4].wait()

        lane16 = lax.broadcasted_iota(jnp.int32, (PAIRS, 128), 1)

        def tile(t, c):
            b = jnp.minimum(jnp.maximum(tsm[t, 0], 0), BLOCKS - 1)
            at = pl.ds(pl.multiple_of(t * PAIRS, PAIRS), PAIRS)
            q = jnp.concatenate([qs[h, at, :] for h in range(HEADS)], axis=0)
            sc = nt(keys[b], q) * SCALE2
            mh, ml = split(jnp.max(sc, axis=0, keepdims=True))
            m = mh + ml
            e = jnp.exp2(sc - m)
            u = tn(e.astype(BF16), vals[b])
            mt = jnp.broadcast_to(m, (128, 128)).T
            info = jnp.zeros((PAIRS, 128), F32)
            for h in range(HEADS):
                rows = slice(h * PAIRS, (h + 1) * PAIRS)
                us[at, h * HD:(h + 1) * HD] = u[rows, 0:HD].astype(BF16)
                info = jnp.where(lane16 == h, mt[rows], info)
                info = jnp.where(lane16 == 8 + h, u[rows, HD:VW], info)
            hi, lo = split(info)
            us[at, QW:QW + 128] = (hi + pltpu.roll(lo, 16, 1)).astype(BF16)
            return c

        lax.fori_loop(0, TILES, tile, 0, unroll=32)

        lane = lax.broadcasted_iota(jnp.int32, (ROWS, 128), 1)
        head = lane < HEADS
        info = mm(g01[...], us[:, QW:QW + 128])
        m01, l01 = [], []
        for c in range(2):
            f = info[c * ROWS:(c + 1) * ROWS]
            f = f + pltpu.roll(f, 112, 1)
            m01.append(jnp.where(head & (live01[c] > 0.5), f, LOW))
            l01.append(pltpu.roll(f, 120, 1))
        m = jnp.maximum(m01[0], m01[1])
        w01 = [jnp.where(head & (live01[c] > 0.5), jnp.exp2(m01[c] - m), 0.0) for c in range(2)]
        l = jnp.where(head, w01[0] * l01[0] + w01[1] * l01[1], 0.0)
        hi, lo = split(jnp.where(head, m, 0.0) + pltpu.roll(l, 8, 1))
        packed = hi + pltpu.roll(lo, 16, 1)
        asend[:, :, QW:QW + 128] = packed.reshape(16, LOC, 128).astype(BF16)
        for h in range(0, HEADS, 2):
            both = mm(g01[...], us[:, h * HD:(h + 2) * HD])
            for k in range(2):
                cols = slice(k * HD, (k + 1) * HD)
                at = slice((h + k) * HD, (h + k + 1) * HD)
                u = both[0:ROWS, cols] * w01[0][:, h + k:h + k + 1]
                u = u + both[ROWS:, cols] * w01[1][:, h + k:h + k + 1]
                asend[:, :, at] = u.reshape(16, LOC, HD).astype(BF16)
        to_all_kv(lambda d, dst: send(asend.at[dst], arecv.at[d - 1], PART, dst, tp))
        sent(qall.at[pl.ds(0, 15)], AGQ)

        lane8 = lax.broadcasted_iota(jnp.int32, (LOC, 128), 1)
        head8 = lane8 < HEADS
        tmc = jnp.full((LOC, 128), LOW, F32)
        tlc = jnp.zeros((LOC, 128), F32)
        for h in range(HEADS):
            tmc = jnp.where(lane8 == h, tm[h * LOC:(h + 1) * LOC], tmc)
            tlc = jnp.where(lane8 == h, tl[h * LOC:(h + 1) * LOC], tlc)
        arecv[15] = asend[me]
        got(arecv.at[pl.ds(0, 15)], PART)
        ms, lsum = [], []
        top = tmc
        for o in range(16):
            f = arecv[o, :, QW:QW + 128].astype(F32)
            f = f + pltpu.roll(f, 112, 1)
            m = jnp.where(head8, f, LOW)
            ms.append(m)
            lsum.append(pltpu.roll(f, 120, 1))
            top = jnp.maximum(top, m)
        wt = jnp.exp2(tmc - top)
        wo_ = [jnp.exp2(m - top) for m in ms]
        den = wt * tlc
        for o in range(16):
            den = den + wo_[o] * lsum[o]
        inv = jnp.where(head8, 1.0 / jnp.where(head8, den, 1.0), 0.0)
        wt = wt * inv
        wo_ = [w * inv for w in wo_]
        for h in range(HEADS):
            o_h = wt[:, h:h + 1] * tu[h * LOC:(h + 1) * LOC]
            for o in range(16):
                o_h = o_h + wo_[o][:, h:h + 1] * arecv[o, :, h * HD:(h + 1) * HD].astype(F32)
            oall[me, :, h * HD:(h + 1) * HD] = o_h.astype(BF16)
        to_all_kv(lambda d, dst: send(oall.at[me], oall.at[me], AGO, dst, tp))
        sent(arecv.at[pl.ds(0, 15)], PART)

        @pl.when(s == 0)
        def _():
            loads[5].wait()

        got(oall.at[pl.ds(0, 15)], AGO)
        oa = oall[...].astype(F32).reshape(ROWS, QW).astype(BF16)
        tp_sum(mm(oa, wo[...]), TA, xra, xb, hb)

        hf = hb[...].astype(F32).reshape(ROWS, WD)
        a2 = (hf * gain2[...]).astype(BF16)

        @pl.when(s == 0)
        def _():
            loads[6].wait()
            for load in ups:
                load.wait()

        subs = [pl.ds(*sub) for sub in SUBS]
        lo, hi = subs
        yp, ym, zp, zm = [lax.rem(v + k, 4) for v in (y, z) for k in (1, 3)]
        y2, z2 = lax.rem(y + 2, 4), lax.rem(z + 2, 4)

        def at_y(t):
            return t * 4 + z

        def at_z(t):
            return y * 4 + t

        for off in (2, 1, 3, 0):
            yk = lax.rem(y + off, 4)
            zk = lax.rem(z + off, 4)
            rows = pl.ds(pl.multiple_of(yk * (4 * CH), 16), 4 * CH)
            for own, there, into, relay, sem, rsm, dev, far, plus, minus in (
                (gs, yk, g1r, rlg, G1, RG, at_z, z2, zp, zm),
                (up, zk, u1r, rlu, U1, RU, at_y, y2, yp, ym),
            ):
                w = wg[rows, :] if own is gs else wu[zk].reshape(4 * CH, WD)
                own[there] = nt(w, a2).reshape(4, CH, ROWS).astype(BF16)
                if off > 0:
                    e = off - 1
                    send(own.at[there, far, lo], relay.at[e, lo], rsm[e], dev(plus), tp)
                    send(own.at[there, far, hi], relay.at[e, hi], rsm[e], dev(minus), tp)
                    send(own.at[there, plus, hi], into.at[off, 0, hi], sem[off], dev(plus), tp)
                    send(own.at[there, minus, lo], into.at[off, 2, lo], sem[off], dev(minus), tp)
                else:
                    for k, t in ((2, far), (1, plus), (3, minus)):
                        send(own.at[there, t], into.at[0, k - 1], sem[0], dev(t), tp)
            if off == 2:
                sent(oall.at[pl.ds(0, 15)], AGO)
                sent(hb.at[0], TA[2])
                sq = jnp.sum(hf * hf, axis=1, keepdims=True)
                sqs[...] = jnp.broadcast_to(sq, (ROWS, 128)).T[0:8]
                to_all_kv(lambda d, dst: send(sqs, sqr.at[d - 1], SQR, dst, tp))
        for off in (2, 1, 3):
            yk = lax.rem(y + off, 4)
            zk = lax.rem(z + off, 4)
            e = off - 1
            for own, there, into, relay, both, sem, rsm, dev, plus, minus in (
                (gs, yk, g1r, rlg, crg, G1, RG, at_z, zp, zm),
                (up, zk, u1r, rlu, cru, U1, RU, at_y, yp, ym),
            ):
                got(relay.at[e], rsm[e])
                v = own[there, plus, lo, :].astype(F32) + relay[e, lo, :].astype(F32)
                both[e, lo, :] = v.astype(BF16)
                send(both.at[e, lo], into.at[off, 0, lo], sem[off], dev(plus), tp)
                v = own[there, minus, hi, :].astype(F32) + relay[e, hi, :].astype(F32)
                both[e, hi, :] = v.astype(BF16)
                send(both.at[e, hi], into.at[off, 2, hi], sem[off], dev(minus), tp)
        for off in (2, 1, 3, 0):
            yk = lax.rem(y + off, 4)
            zk = lax.rem(z + off, 4)
            parts = (0, 2) if off > 0 else (0, 1, 2)
            got(g1r.at[off, pl.ds(0, len(parts))], G1[off])
            gate = gs[yk, z].astype(F32)
            for d in parts:
                gate = gate + g1r[off, d].astype(F32)
            if off > 0:
                g1s[off - 1] = gate.astype(BF16)
                send(g1s.at[off - 1], g2r.at[off - 1], G2, at_y(yk), tp)
            got(u1r.at[off, pl.ds(0, len(parts))], U1[off])
            upv = up[zk, y].astype(F32)
            for d in parts:
                upv = upv + u1r[off, d].astype(F32)
            if off > 0:
                u1s[off - 1] = upv.astype(BF16)
                send(u1s.at[off - 1], u2r.at[off - 1], U2, at_z(zk), tp)
        got(sqr, SQR)
        sqt = sqs[...]
        for d in range(15):
            sqt = sqt + sqr[d]
        factor = lax.rsqrt(sqt / D + EPS)[0:1]
        got(g2r, G2)
        got(u2r, U2)
        for d in range(3):
            gate = gate + g2r[d].astype(F32)
            upv = upv + u2r[d].astype(F32)
        gate = gate * factor
        upv = upv * factor
        ug[y, z] = (gate / (1.0 + jnp.exp(-gate)) * upv).astype(BF16)

        first, second = ug.at[y, z, subs[0]], ug.at[y, z, subs[1]]
        for k in (2, 1, 3):
            send(first, first, A1[k - 1], lax.rem(y + k, 4) * 4 + z, tp)
            send(second, second, B1[k - 1], y * 4 + lax.rem(z + k, 4), tp)
        for k in (2, 1, 3):
            send(first, first, A2[k - 1], y * 4 + lax.rem(z + k, 4), tp)
            send(second, second, B2[k - 1], lax.rem(y + k, 4) * 4 + z, tp)
        for d in (1, 3, 2):
            slab = ug.at[lax.rem(y + 4 - d, 4), z, subs[0]]
            got(slab, A1[d - 1])
            for k in (2, 1, 3):
                send(slab, slab, A2[k - 1], y * 4 + lax.rem(z + k, 4), tp)
            slab = ug.at[y, lax.rem(z + 4 - d, 4), subs[1]]
            got(slab, B1[d - 1])
            for k in (2, 1, 3):
                send(slab, slab, B2[k - 1], lax.rem(y + k, 4) * 4 + z, tp)
        sent(sqr, SQR)
        for off in range(4):
            n = 3 if off == 0 else 2
            sent(g1r.at[off, pl.ds(0, n)], G1[off])
            sent(u1r.at[off, pl.ds(0, n)], U1[off])
        for e in range(3):
            sent(rlg.at[e], RG[e])
            sent(rlu.at[e], RU[e])
        sent(g2r, G2)
        sent(u2r, U2)

        @pl.when(s == 0)
        def _():
            loads[7].wait()

        def down(c, at):
            lo, n = SUBS[c]
            spots = [(t, at) if c == 0 else (at, t) for t in range(4)]
            u = [ug[i, j, lo:lo + n, :] for i, j in spots]
            w = [ws[pl.ds(pl.multiple_of((i * 4 + j) * CH + lo, 16), n), :] for i, j in spots]
            return mm(jnp.concatenate(u, axis=0).T, jnp.concatenate(w, axis=0))

        acc[...] = down(0, z)
        acc[...] += down(1, y)
        for d in (1, 3, 2):
            got(ug.at[:, 0, subs[0]], A2[d - 1])
            acc[...] += down(0, lax.rem(z + 4 - d, 4))
            got(ug.at[0, :, subs[1]], B2[d - 1])
            acc[...] += down(1, lax.rem(y + 4 - d, 4))
        for d in range(3):
            sent(first, A1[d])
            sent(second, B1[d])
            sent(ug.at[:, 0, subs[0]], A2[d])
            sent(ug.at[0, :, subs[1]], B2[d])
        tp_sum(acc[...], TB, xrb, hb, xb)

        @pl.when(s < STEPS - 1)
        def _():
            project()

        return carry

    lax.fori_loop(0, STEPS, step, 0)
    sent(xb.at[0], TB[2])
    x_out[...] = xb[...]


def layer(x, gain1, wi, bias, wo, gain2, we, ws, pc, tc, tlen, idx, cnt):
    vmem = pl.BlockSpec(memory_space=pltpu.VMEM)
    smem = pl.BlockSpec(memory_space=pltpu.SMEM)
    hbm = pl.BlockSpec(memory_space=pl.ANY)
    b = lambda *shape: pltpu.VMEM(shape, BF16)
    f = lambda *shape: pltpu.VMEM(shape, F32)
    i = lambda *shape: pltpu.VMEM(shape, jnp.int32)
    return pl.pallas_call(
        kernel,
        out_shape=[
            jax.ShapeDtypeStruct((2, 64, WD), BF16),
            jax.ShapeDtypeStruct((2, STEPS, LOC, HD), BF16),
        ],
        in_specs=[hbm, vmem, hbm, vmem, hbm, vmem, hbm, hbm, hbm, hbm, smem, vmem, vmem],
        out_specs=[vmem, vmem],
        scratch_shapes=[
            b(2, 64, WD), b(2, 64, WD),
            b(WD, PW), b(QW, WD), b(FFP, WD), b(4, 4, CH, WD), b(FFP, WD),
            b(BLOCKS, BLOCK, HD), b(BLOCKS, BLOCK, VW), b(2, LOC, TAIL, HD),
            i(3, LOC, 128), i(16, 3, LOC, 128), pltpu.SMEM((TILES, 128), jnp.int32), i(TILES, 128),
            b(2 * ROWS, SLOTS), b(SLOTS, ROWS), f(2, ROWS, 128),
            b(16, LOC, PW + 128), b(15, LOC, PW + 128), b(LOC, PW),
            b(16, LOC, QW), b(HEADS, SLOTS, HD), b(SLOTS, QW + 128),
            b(16, LOC, QW + 128), b(16, LOC, QW + 128), b(16, LOC, QW),
            b(2, 64, WD), b(64, WD), b(4, 64, WD), b(4, 64, WD),
            f(8, 128), f(15, 8, 128),
            b(4, 4, CH, ROWS), b(4, 4, CH, ROWS),
            b(3, CH, ROWS), b(3, CH, ROWS), b(3, CH, ROWS), b(3, CH, ROWS),
            b(4, 3, CH, ROWS), b(4, 3, CH, ROWS),
            b(3, CH, ROWS), b(3, CH, ROWS), b(3, CH, ROWS), b(3, CH, ROWS),
            b(4, 4, CH, ROWS), f(ROWS, WD), f(HEADS * LOC, TAIL),
            pltpu.SemaphoreType.DMA((24,)),
            pltpu.SemaphoreType.DMA((N_SEM,)),
            pltpu.SemaphoreType.DMA((N_SEM,)),
        ],
        compiler_params=pltpu.CompilerParams(
            collective_id=0, has_side_effects=True, vmem_limit_bytes=56 * 1024 * 1024
        ),
        name="layer",
    )(x, gain1, wi, bias, wo, gain2, we, ws, pc, tc, tlen, idx, cnt)


def copies(x, cache, x_out, cache_out):
    x_out[...] = x[...]
    cache_out[...] = cache[...]


def write(x, cache):
    vmem = pl.BlockSpec(memory_space=pltpu.VMEM)
    return pl.pallas_call(
        copies,
        out_shape=[jax.ShapeDtypeStruct(x.shape, x.dtype), jax.ShapeDtypeStruct(cache.shape, cache.dtype)],
        in_specs=[vmem, vmem],
        out_specs=[vmem, vmem],
        name="write",
    )(x, cache)


def local(
    states, first_gain, input_weight, input_bias, output_weight, second_gain, expand_weight,
    shrink_weight, prompt_cache, tail_cache, tail_length, block_index, block_count,
):
    x, cache = layer(
        states.reshape(2, 64, WD),
        first_gain.reshape(1, WD),
        input_weight.reshape(WD, PW),
        input_bias.reshape(1, PW),
        output_weight.reshape(QW, WD),
        second_gain.reshape(1, WD),
        jnp.transpose(expand_weight, (1, 2, 0)),
        shrink_weight,
        prompt_cache.reshape(2, BLOCKS, BLOCK, HD),
        tail_cache.reshape(2, LOC, TAIL, HD),
        tail_length,
        jnp.transpose(block_index[:, 0], (0, 2, 1)),
        block_count,
    )
    x, cache = write(x, cache)
    cache = jnp.transpose(cache, (0, 2, 1, 3)).reshape(2, LOC, STEPS, 1, HD)
    return (x.reshape(ROWS, WD), cache)


def solution(mesh):
    return jax.shard_map(
        local,
        mesh=mesh,
        in_specs=(
            P(None, "kv"),
            P("kv"),
            P("kv", "tp", None),
            P("tp", None),
            P("tp", None, "kv"),
            P("kv"),
            P("kv", None, "tp"),
            P("tp", "kv"),
            P(None, "tp", "kv", None, None),
            P(None, "kv", None, "tp", None),
            P("kv"),
            P("kv", "tp", None, None),
            P("kv", "tp", None),
        ),
        out_specs=(P(None, "kv"), P(None, "kv", None, "tp", None)),
        check_vma=False,
    )
```

```python
import functools

import jax
import jax.numpy as jnp
from jax import lax
from jax.experimental import pallas as pl
from jax.experimental.pallas import tpu as pltpu
from jax.sharding import PartitionSpec as P

D = 8192
STEPS = 3
ROWS = 128
LOC = 8
HEADS = 8
HD = 128
QW = HEADS * HD
PW = QW + 2 * HD
BLOCKS = 16
BLOCK = 512
TAIL = 512
FF = 3696
CH = 240
FFP = 16 * CH
WD = 512
TILES = 32
PAIRS = 16
SLOTS = TILES * PAIRS
EPS = 1e-06
LOW = -1e30
SCALE = HD ** (-0.5)
SCALE2 = SCALE * 1.4426950408889634
VW = 2 * HD
F32 = jnp.float32
BF16 = jnp.bfloat16
MESH = pl.DeviceIdType.MESH

(TBL, RSP, AGQ, PART, AGO, TRA, TGA, SQR, TRB, TGB, G2, U2) = range(12)
A1, B1, A2, B2 = (12, 13, 14), (15, 16, 17), (18, 19, 20), (21, 22, 23)
G1, U1 = (24, 25, 26, 27), (28, 29, 30, 31)
RG, RU = (32, 33, 34), (35, 36, 37)
TA, TB = (TRA, TGA, 38), (TRB, TGB, 39)
N_SEM = 40
SUBS = ((0, 128), (128, CH - 128))
KV_ORDER = ((2, 2), (1, 2), (2, 1), (3, 2), (2, 3), (0, 2), (2, 0), (1, 1), (3, 3), (1, 3), (3, 1),
            (0, 1), (1, 0), (0, 3), (3, 0))
TP_ORDER = (4, 3, 5, 2, 6, 1, 7)


def nt(a, b):
    return lax.dot_general(a, b, (((1,), (1,)), ((), ())), preferred_element_type=F32)


def tn(a, b):
    return lax.dot_general(a, b, (((0,), (0,)), ((), ())), preferred_element_type=F32)


def mm(a, b):
    return jnp.dot(a, b, preferred_element_type=F32)


def split(v):
    hi = v.astype(BF16).astype(F32)
    lo = (v - hi).astype(BF16).astype(F32)
    return hi, lo


def kernel(
    x_hbm, gain1, wi_hbm, bias, wo_hbm, gain2, we_hbm, ws_hbm, pc_hbm, tc_hbm, tlen, idx, cnt,
    x_out, cache_out,
    xb, hb, wi, wo, wg, wu, ws, keys, vals, tail,
    table, tb, tsm, tvm, g01, gm, live01,
    ps, pr, pqkv, qall, qs, us, asend, arecv, oall,
    ys, sib, xra, xrb, sqs, sqr, gs, up, rlg, rlu, crg, cru, g1r, u1r, g1s, u1s, g2r, u2r, ug, acc, tlmask,
    wsem, ssem, rsem,
):
    me = lax.axis_index("kv")
    tp = lax.axis_index("tp")
    y = lax.div(me, 4)
    z = lax.rem(me, 4)

    def kv_at(dy, dz):
        return lax.rem(y + dy, 4) * 4 + lax.rem(z + dz, 4)

    def send(src, dst, ph, to_kv, to_tp):
        pltpu.make_async_remote_copy(
            src_ref=src, dst_ref=dst, send_sem=ssem.at[ph], recv_sem=rsem.at[ph],
            device_id=(to_kv, to_tp), device_id_type=MESH,
        ).start()

    def got(ref, ph):
        pltpu.make_async_copy(ref, ref, rsem.at[ph]).wait()

    def sent(ref, ph):
        pltpu.make_async_copy(ref, ref, ssem.at[ph]).wait()

    def to_all_kv(fn):
        for dy, dz in KV_ORDER:
            fn(4 * dy + dz, kv_at(dy, dz))

    def to_all_tp(fn):
        for d in TP_ORDER:
            fn(d, lax.rem(tp + d, 8))

    barrier = pltpu.get_barrier_semaphore()
    to_all_kv(lambda d, dst: pl.semaphore_signal(
        barrier, inc=1, device_id=(dst, tp), device_id_type=MESH))
    to_all_tp(lambda d, dst: pl.semaphore_signal(
        barrier, inc=1, device_id=(me, dst), device_id_type=MESH))

    def up_rows(i):
        n = min(CH, FF - i * CH)
        return pltpu.make_async_copy(
            we_hbm.at[1, pl.ds(i * CH, n)], wu.at[i % 4, i // 4, pl.ds(0, n)], wsem.at[8 + i])

    loads = [
        pltpu.make_async_copy(x_hbm, xb, wsem.at[0]),
        pltpu.make_async_copy(wi_hbm, wi, wsem.at[1]),
        pltpu.make_async_copy(tc_hbm, tail, wsem.at[2]),
        pltpu.make_async_copy(pc_hbm.at[0], keys, wsem.at[3]),
        pltpu.make_async_copy(pc_hbm.at[1], vals.at[:, :, pl.ds(0, HD)], wsem.at[4]),
        pltpu.make_async_copy(wo_hbm, wo, wsem.at[5]),
        pltpu.make_async_copy(we_hbm.at[0], wg.at[pl.ds(0, FF)], wsem.at[6]),
        pltpu.make_async_copy(ws_hbm, ws.at[pl.ds(0, FF)], wsem.at[7]),
    ]
    ups = [up_rows(i) for i in range(16)]
    for load in loads + ups:
        load.start()

    table[...] = jnp.zeros_like(table)
    table[0, :, 0:16] = idx[:, 0, :]
    table[1, :, 0:16] = idx[:, 1, :]
    table[2, :, 0:16] = cnt[:, 0, :]
    tb[me] = table[...]

    def project():
        xf = xb[...].astype(F32).reshape(ROWS, WD)
        sq = jnp.sum(xf * xf, axis=1, keepdims=True)
        a = (xf * gain1[...]).astype(BF16)
        ps[:, :, 0:PW] = mm(a, wi[...]).reshape(16, LOC, PW).astype(BF16)
        hi, lo = split(sq)
        half = lax.broadcasted_iota(jnp.int32, (ROWS, 128), 1) < 64
        ps[:, :, PW:PW + 128] = jnp.where(half, hi, lo).reshape(16, LOC, 128).astype(BF16)

    wg[FF:FFP, :] = jnp.zeros((FFP - FF, WD), BF16)
    wu[3, 3, FF - 15 * CH:CH, :] = jnp.zeros((FFP - FF, WD), BF16)
    vals[:, :, HD:VW] = jnp.ones((BLOCKS, BLOCK, HD), BF16)
    ws[FF:FFP, :] = jnp.zeros((FFP - FF, WD), BF16)
    cache_out[...] = jnp.zeros_like(cache_out)
    rowmod = lax.rem(lax.broadcasted_iota(jnp.int32, (HEADS * LOC, TAIL), 0), LOC)
    tlm = jnp.zeros((HEADS * LOC, TAIL), jnp.int32)
    for r in range(LOC):
        tlm = jnp.where(rowmod == r, tlen[r], tlm)
    tpos = lax.broadcasted_iota(jnp.int32, (HEADS * LOC, TAIL), 1)
    tlmask[...] = (tpos < tlm).astype(F32)

    loads[0].wait()
    loads[1].wait()
    project()
    pl.semaphore_wait(barrier, 22)

    def sort_pairs():
        lane = lax.broadcasted_iota(jnp.int32, (ROWS, 128), 1)
        row = lax.broadcasted_iota(jnp.int32, (ROWS, 128), 0)
        valid = lane < BLOCKS
        b0, b1, n = [
            jnp.sum(jnp.where(lane == me, tb[:, k].reshape(ROWS, 128).astype(F32), 0.0),
                    axis=1, keepdims=True).astype(jnp.int32) for k in range(3)
        ]
        e0 = jnp.where((b0 == lane) & (n > 0) & valid, 1.0, 0.0).astype(F32)
        e1 = jnp.where((b1 == lane) & (n > 1) & valid, 1.0, 0.0).astype(F32)
        lower = jnp.where(lane < row, 1.0, 0.0).astype(BF16)
        c0 = mm(lower, e0.astype(BF16))
        c1 = mm(lower, e1.astype(BF16))
        n0 = jnp.sum(e0, axis=0, keepdims=True)
        n1 = jnp.sum(e1, axis=0, keepdims=True)
        n = (n0 + n1).astype(jnp.int32)
        ntile = lax.shift_right_logical(n + (PAIRS - 1), 4).astype(F32)
        upper = jnp.where(row < lane, 1.0, 0.0).astype(BF16)
        nt8 = jnp.broadcast_to(ntile, (8, 128))
        tstart = mm(nt8.astype(BF16), upper)[0:1]
        p0 = jnp.sum(e0 * (PAIRS * tstart + c0), axis=1, keepdims=True)
        p1 = jnp.sum(e1 * (PAIRS * tstart + n0 + c1), axis=1, keepdims=True)
        l0 = jnp.sum(e0, axis=1, keepdims=True)
        l1 = jnp.sum(e1, axis=1, keepdims=True)
        p0 = jnp.where(l0 > 0.5, p0, -1.0).astype(jnp.int32)
        p1 = jnp.where(l1 > 0.5, p1, -1.0).astype(jnp.int32)
        live01[0] = jnp.broadcast_to(l0, (ROWS, 128))
        live01[1] = jnp.broadcast_to(l1, (ROWS, 128))
        slot = lax.broadcasted_iota(jnp.int32, (ROWS, SLOTS), 1)
        h0 = jnp.where(p0 == slot, 1.0, 0.0).astype(F32)
        h1 = jnp.where(p1 == slot, 1.0, 0.0).astype(F32)
        g01[0:ROWS] = h0.astype(BF16)
        g01[ROWS:2 * ROWS] = h1.astype(BF16)
        gm[...] = (h0 + h1).T.astype(BF16)
        tend = tstart + ntile
        ti = lax.broadcasted_iota(jnp.int32, (TILES, 128), 0).astype(F32)
        tl = lax.broadcasted_iota(jnp.int32, (TILES, 128), 1)
        done = jnp.where((tl < BLOCKS) & (tend <= ti), 1.0, 0.0).astype(F32)
        cnt = jnp.minimum(jnp.sum(done, axis=1, keepdims=True), BLOCKS - 1.0)
        tvm[...] = jnp.broadcast_to(cnt, (TILES, 128)).astype(jnp.int32)
        pltpu.sync_copy(tvm, tsm)

    core = lax.rem(tp, 2)
    chip = lax.div(tp, 2)
    sibling = tp + 1 - 2 * core

    def tp_sum(part, ph, xr, res, dst):
        ys[...] = part.reshape(2, 64, WD).astype(BF16)
        send(ys.at[1 - core], sib, ph[0], me, sibling)
        own = ys[core].astype(F32)
        got(sib, ph[0])
        xr[chip] = (own + sib[...].astype(F32)).astype(BF16)
        for d in (2, 1, 3):
            send(xr.at[chip], xr.at[chip], ph[1], me, lax.rem(tp + 2 * d, 8))
        sent(sib, ph[0])
        got(xr.at[pl.ds(0, 3)], ph[1])
        total = xr[0].astype(F32)
        for d in range(1, 4):
            total = total + xr[d].astype(F32)
        dst[core] = (res[core].astype(F32) + total.astype(BF16).astype(F32)).astype(BF16)
        send(dst.at[core], dst.at[core], ph[2], me, sibling)
        sent(xr.at[pl.ds(0, 3)], ph[1])
        got(dst.at[0], ph[2])

    def step(s, carry):
        to_all_kv(lambda d, dst: send(ps.at[dst], pr.at[d - 1], RSP, dst, tp))

        @pl.when(s == 0)
        def _():
            to_all_kv(lambda d, dst: send(table, tb.at[me], TBL, dst, tp))

        @pl.when(s > 0)
        def _():
            sent(xb.at[0], TB[2])


        total = ps[me].astype(F32)
        got(pr, RSP)
        for d in range(15):
            total = total + pr[d].astype(F32)
        factor = lax.rsqrt((total[:, PW:PW + 1] + total[:, PW + 64:PW + 65]) / D + EPS)
        proj = (total[:, 0:PW] * factor + bias[...].astype(F32)).astype(BF16)
        pqkv[...] = proj
        cache_out[0, s] = proj[:, QW:QW + HD]
        cache_out[1, s] = proj[:, QW + HD:QW + 2 * HD]
        qall[me] = proj[:, 0:QW]
        to_all_kv(lambda d, dst: send(qall.at[me], qall.at[me], AGQ, dst, tp))
        sent(pr, RSP)

        @pl.when(s == 0)
        def _():
            got(tb.at[pl.ds(0, 15)], TBL)
            sent(tb.at[pl.ds(0, 15)], TBL)
            sort_pairs()
            loads[2].wait()

        pf = pqkv[...].astype(F32)
        qh = jnp.concatenate([pf[:, h * HD:(h + 1) * HD] for h in range(HEADS)], axis=0)
        qhb = qh.astype(BF16)
        rm = lax.rem(lax.broadcasted_iota(jnp.int32, (HEADS * LOC, TAIL), 0), LOC)
        sc = jnp.zeros((HEADS * LOC, TAIL), F32)
        for r in range(LOC):
            sc = jnp.where(rm == r, nt(qhb, tail[0, r]), sc)
        sc = sc * SCALE2
        tmask = tlmask[...] > 0.5
        sc = jnp.where(tmask, sc, LOW)
        fresh = []
        for t in range(STEPS):
            kf = cache_out[0, t].astype(F32)
            kf = jnp.concatenate([kf] * HEADS, axis=0)
            f = jnp.sum(qh * kf, axis=1, keepdims=True) * SCALE2
            fresh.append(jnp.where(t <= s, f, LOW))
        tm = jnp.max(sc, axis=1, keepdims=True)
        for f in fresh:
            tm = jnp.maximum(tm, f)
        e = jnp.where(tmask, jnp.exp2(sc - tm), 0.0)
        tl = jnp.sum(e, axis=1, keepdims=True)
        eb = e.astype(BF16)
        tu = jnp.zeros((HEADS * LOC, HD), F32)
        for r in range(LOC):
            tu = tu + mm(jnp.where(rm == r, eb, jnp.zeros_like(eb)), tail[1, r])
        for t in range(STEPS):
            ef = jnp.where(t <= s, jnp.exp2(fresh[t] - tm), 0.0)
            tl = tl + ef
            vf = cache_out[1, t].astype(F32)
            tu = tu + ef.astype(BF16).astype(F32) * jnp.concatenate([vf] * HEADS, axis=0)

        got(qall.at[pl.ds(0, 15)], AGQ)
        for h in range(0, HEADS, 2):
            qa = qall[:, :, h * HD:(h + 2) * HD].astype(F32).reshape(ROWS, 2 * HD).astype(BF16)
            both = mm(gm[...], qa).astype(BF16)
            qs[h] = both[:, 0:HD]
            qs[h + 1] = both[:, HD:2 * HD]

        @pl.when(s == 0)
        def _():
            loads[3].wait()
            loads[4].wait()

        lane16 = lax.broadcasted_iota(jnp.int32, (PAIRS, 128), 1)

        def tile(t, c):
            b = jnp.minimum(jnp.maximum(tsm[t, 0], 0), BLOCKS - 1)
            at = pl.ds(pl.multiple_of(t * PAIRS, PAIRS), PAIRS)
            q = jnp.concatenate([qs[h, at, :] for h in range(HEADS)], axis=0)
            sc = nt(keys[b], q) * SCALE2
            mh, ml = split(jnp.max(sc, axis=0, keepdims=True))
            m = mh + ml
            e = jnp.exp2(sc - m)
            u = tn(e.astype(BF16), vals[b])
            mt = jnp.broadcast_to(m, (128, 128)).T
            info = jnp.zeros((PAIRS, 128), F32)
            for h in range(HEADS):
                rows = slice(h * PAIRS, (h + 1) * PAIRS)
                us[at, h * HD:(h + 1) * HD] = u[rows, 0:HD].astype(BF16)
                info = jnp.where(lane16 == h, mt[rows], info)
                info = jnp.where(lane16 == 8 + h, u[rows, HD:VW], info)
            hi, lo = split(info)
            us[at, QW:QW + 128] = (hi + pltpu.roll(lo, 16, 1)).astype(BF16)
            return c

        lax.fori_loop(0, TILES, tile, 0, unroll=32)

        lane = lax.broadcasted_iota(jnp.int32, (ROWS, 128), 1)
        head = lane < HEADS
        info = mm(g01[...], us[:, QW:QW + 128])
        m01, l01 = [], []
        for c in range(2):
            f = info[c * ROWS:(c + 1) * ROWS]
            f = f + pltpu.roll(f, 112, 1)
            m01.append(jnp.where(head & (live01[c] > 0.5), f, LOW))
            l01.append(pltpu.roll(f, 120, 1))
        m = jnp.maximum(m01[0], m01[1])
        w01 = [jnp.where(head & (live01[c] > 0.5), jnp.exp2(m01[c] - m), 0.0) for c in range(2)]
        l = jnp.where(head, w01[0] * l01[0] + w01[1] * l01[1], 0.0)
        hi, lo = split(jnp.where(head, m, 0.0) + pltpu.roll(l, 8, 1))
        packed = hi + pltpu.roll(lo, 16, 1)
        asend[:, :, QW:QW + 128] = packed.reshape(16, LOC, 128).astype(BF16)
        for h in range(0, HEADS, 2):
            both = mm(g01[...], us[:, h * HD:(h + 2) * HD])
            for k in range(2):
                cols = slice(k * HD, (k + 1) * HD)
                at = slice((h + k) * HD, (h + k + 1) * HD)
                u = both[0:ROWS, cols] * w01[0][:, h + k:h + k + 1]
                u = u + both[ROWS:, cols] * w01[1][:, h + k:h + k + 1]
                asend[:, :, at] = u.reshape(16, LOC, HD).astype(BF16)
        to_all_kv(lambda d, dst: send(asend.at[dst], arecv.at[d - 1], PART, dst, tp))
        sent(qall.at[pl.ds(0, 15)], AGQ)

        lane8 = lax.broadcasted_iota(jnp.int32, (LOC, 128), 1)
        head8 = lane8 < HEADS
        tmc = jnp.full((LOC, 128), LOW, F32)
        tlc = jnp.zeros((LOC, 128), F32)
        for h in range(HEADS):
            tmc = jnp.where(lane8 == h, tm[h * LOC:(h + 1) * LOC], tmc)
            tlc = jnp.where(lane8 == h, tl[h * LOC:(h + 1) * LOC], tlc)
        arecv[15] = asend[me]
        got(arecv.at[pl.ds(0, 15)], PART)
        ms, lsum = [], []
        top = tmc
        for o in range(16):
            f = arecv[o, :, QW:QW + 128].astype(F32)
            f = f + pltpu.roll(f, 112, 1)
            m = jnp.where(head8, f, LOW)
            ms.append(m)
            lsum.append(pltpu.roll(f, 120, 1))
            top = jnp.maximum(top, m)
        wt = jnp.exp2(tmc - top)
        wo_ = [jnp.exp2(m - top) for m in ms]
        den = wt * tlc
        for o in range(16):
            den = den + wo_[o] * lsum[o]
        inv = jnp.where(head8, 1.0 / jnp.where(head8, den, 1.0), 0.0)
        wt = wt * inv
        wo_ = [w * inv for w in wo_]
        for h in range(HEADS):
            o_h = wt[:, h:h + 1] * tu[h * LOC:(h + 1) * LOC]
            for o in range(16):
                o_h = o_h + wo_[o][:, h:h + 1] * arecv[o, :, h * HD:(h + 1) * HD].astype(F32)
            oall[me, :, h * HD:(h + 1) * HD] = o_h.astype(BF16)
        to_all_kv(lambda d, dst: send(oall.at[me], oall.at[me], AGO, dst, tp))
        sent(arecv.at[pl.ds(0, 15)], PART)

        @pl.when(s == 0)
        def _():
            loads[5].wait()

        got(oall.at[pl.ds(0, 15)], AGO)
        oa = oall[...].astype(F32).reshape(ROWS, QW).astype(BF16)
        tp_sum(mm(oa, wo[...]), TA, xra, xb, hb)

        hf = hb[...].astype(F32).reshape(ROWS, WD)
        a2 = (hf * gain2[...]).astype(BF16)

        @pl.when(s == 0)
        def _():
            loads[6].wait()
            for load in ups:
                load.wait()

        subs = [pl.ds(*sub) for sub in SUBS]
        lo, hi = subs
        yp, ym, zp, zm = [lax.rem(v + k, 4) for v in (y, z) for k in (1, 3)]
        y2, z2 = lax.rem(y + 2, 4), lax.rem(z + 2, 4)

        def at_y(t):
            return t * 4 + z

        def at_z(t):
            return y * 4 + t

        for off in (2, 1, 3, 0):
            yk = lax.rem(y + off, 4)
            zk = lax.rem(z + off, 4)
            rows = pl.ds(pl.multiple_of(yk * (4 * CH), 16), 4 * CH)
            for own, there, into, relay, sem, rsm, dev, far, plus, minus in (
                (gs, yk, g1r, rlg, G1, RG, at_z, z2, zp, zm),
                (up, zk, u1r, rlu, U1, RU, at_y, y2, yp, ym),
            ):
                w = wg[rows, :] if own is gs else wu[zk].reshape(4 * CH, WD)
                own[there] = nt(w, a2).reshape(4, CH, ROWS).astype(BF16)
                if off > 0:
                    e = off - 1
                    send(own.at[there, far, lo], relay.at[e, lo], rsm[e], dev(plus), tp)
                    send(own.at[there, far, hi], relay.at[e, hi], rsm[e], dev(minus), tp)
                    send(own.at[there, plus, hi], into.at[off, 0, hi], sem[off], dev(plus), tp)
                    send(own.at[there, minus, lo], into.at[off, 2, lo], sem[off], dev(minus), tp)
                else:
                    for k, t in ((2, far), (1, plus), (3, minus)):
                        send(own.at[there, t], into.at[0, k - 1], sem[0], dev(t), tp)
            if off == 2:
                sent(oall.at[pl.ds(0, 15)], AGO)
                sent(hb.at[0], TA[2])
                sq = jnp.sum(hf * hf, axis=1, keepdims=True)
                sqs[...] = jnp.broadcast_to(sq, (ROWS, 128)).T[0:1]
                to_all_kv(lambda d, dst: send(sqs, sqr.at[d - 1], SQR, dst, tp))
        for off in (2, 1, 3):
            yk = lax.rem(y + off, 4)
            zk = lax.rem(z + off, 4)
            e = off - 1
            for own, there, into, relay, both, sem, rsm, dev, plus, minus in (
                (gs, yk, g1r, rlg, crg, G1, RG, at_z, zp, zm),
                (up, zk, u1r, rlu, cru, U1, RU, at_y, yp, ym),
            ):
                got(relay.at[e], rsm[e])
                v = own[there, plus, lo, :].astype(F32) + relay[e, lo, :].astype(F32)
                both[e, lo, :] = v.astype(BF16)
                send(both.at[e, lo], into.at[off, 0, lo], sem[off], dev(plus), tp)
                v = own[there, minus, hi, :].astype(F32) + relay[e, hi, :].astype(F32)
                both[e, hi, :] = v.astype(BF16)
                send(both.at[e, hi], into.at[off, 2, hi], sem[off], dev(minus), tp)
        for off in (2, 1, 3, 0):
            yk = lax.rem(y + off, 4)
            zk = lax.rem(z + off, 4)
            parts = (0, 2) if off > 0 else (0, 1, 2)
            got(g1r.at[off, pl.ds(0, len(parts))], G1[off])
            gate = gs[yk, z].astype(F32)
            for d in parts:
                gate = gate + g1r[off, d].astype(F32)
            if off > 0:
                g1s[off - 1] = gate.astype(BF16)
                send(g1s.at[off - 1], g2r.at[off - 1], G2, at_y(yk), tp)
            got(u1r.at[off, pl.ds(0, len(parts))], U1[off])
            upv = up[zk, y].astype(F32)
            for d in parts:
                upv = upv + u1r[off, d].astype(F32)
            if off > 0:
                u1s[off - 1] = upv.astype(BF16)
                send(u1s.at[off - 1], u2r.at[off - 1], U2, at_z(zk), tp)
        got(sqr, SQR)
        sqt = sqs[...]
        for d in range(15):
            sqt = sqt + sqr[d]
        factor = lax.rsqrt(sqt / D + EPS)[0:1]
        got(g2r, G2)
        got(u2r, U2)
        for d in range(3):
            gate = gate + g2r[d].astype(F32)
            upv = upv + u2r[d].astype(F32)
        gate = gate * factor
        upv = upv * factor
        ug[y, z] = (gate / (1.0 + jnp.exp(-gate)) * upv).astype(BF16)

        first, second = ug.at[y, z, subs[0]], ug.at[y, z, subs[1]]
        for k in (2, 1, 3):
            send(first, first, A1[k - 1], lax.rem(y + k, 4) * 4 + z, tp)
            send(second, second, B1[k - 1], y * 4 + lax.rem(z + k, 4), tp)
        for k in (2, 1, 3):
            send(first, first, A2[k - 1], y * 4 + lax.rem(z + k, 4), tp)
            send(second, second, B2[k - 1], lax.rem(y + k, 4) * 4 + z, tp)
        for d in (1, 3, 2):
            slab = ug.at[lax.rem(y + 4 - d, 4), z, subs[0]]
            got(slab, A1[d - 1])
            for k in (2, 1, 3):
                send(slab, slab, A2[k - 1], y * 4 + lax.rem(z + k, 4), tp)
            slab = ug.at[y, lax.rem(z + 4 - d, 4), subs[1]]
            got(slab, B1[d - 1])
            for k in (2, 1, 3):
                send(slab, slab, B2[k - 1], lax.rem(y + k, 4) * 4 + z, tp)
        sent(sqr, SQR)
        for off in range(4):
            n = 3 if off == 0 else 2
            sent(g1r.at[off, pl.ds(0, n)], G1[off])
            sent(u1r.at[off, pl.ds(0, n)], U1[off])
        for e in range(3):
            sent(rlg.at[e], RG[e])
            sent(rlu.at[e], RU[e])
        sent(g2r, G2)
        sent(u2r, U2)

        @pl.when(s == 0)
        def _():
            loads[7].wait()

        def down(c, at):
            lo, n = SUBS[c]
            spots = [(t, at) if c == 0 else (at, t) for t in range(4)]
            u = [ug[i, j, lo:lo + n, :] for i, j in spots]
            w = [ws[pl.ds(pl.multiple_of((i * 4 + j) * CH + lo, 16), n), :] for i, j in spots]
            return mm(jnp.concatenate(u, axis=0).T, jnp.concatenate(w, axis=0))

        acc[...] = down(0, z)
        acc[...] += down(1, y)
        for d in (1, 3, 2):
            got(ug.at[:, 0, subs[0]], A2[d - 1])
            acc[...] += down(0, lax.rem(z + 4 - d, 4))
            got(ug.at[0, :, subs[1]], B2[d - 1])
            acc[...] += down(1, lax.rem(y + 4 - d, 4))
        for d in range(3):
            sent(first, A1[d])
            sent(second, B1[d])
            sent(ug.at[:, 0, subs[0]], A2[d])
            sent(ug.at[0, :, subs[1]], B2[d])
        tp_sum(acc[...], TB, xrb, hb, xb)

        @pl.when(s < STEPS - 1)
        def _():
            project()

        return carry

    lax.fori_loop(0, STEPS, step, 0)
    sent(xb.at[0], TB[2])
    x_out[...] = xb[...]


def layer(x, gain1, wi, bias, wo, gain2, we, ws, pc, tc, tlen, idx, cnt):
    vmem = pl.BlockSpec(memory_space=pltpu.VMEM)
    smem = pl.BlockSpec(memory_space=pltpu.SMEM)
    hbm = pl.BlockSpec(memory_space=pl.ANY)
    b = lambda *shape: pltpu.VMEM(shape, BF16)
    f = lambda *shape: pltpu.VMEM(shape, F32)
    i = lambda *shape: pltpu.VMEM(shape, jnp.int32)
    return pl.pallas_call(
        kernel,
        out_shape=[
            jax.ShapeDtypeStruct((2, 64, WD), BF16),
            jax.ShapeDtypeStruct((2, STEPS, LOC, HD), BF16),
        ],
        in_specs=[hbm, vmem, hbm, vmem, hbm, vmem, hbm, hbm, hbm, hbm, smem, vmem, vmem],
        out_specs=[vmem, vmem],
        scratch_shapes=[
            b(2, 64, WD), b(2, 64, WD),
            b(WD, PW), b(QW, WD), b(FFP, WD), b(4, 4, CH, WD), b(FFP, WD),
            b(BLOCKS, BLOCK, HD), b(BLOCKS, BLOCK, VW), b(2, LOC, TAIL, HD),
            i(3, LOC, 128), i(16, 3, LOC, 128), pltpu.SMEM((TILES, 128), jnp.int32), i(TILES, 128),
            b(2 * ROWS, SLOTS), b(SLOTS, ROWS), f(2, ROWS, 128),
            b(16, LOC, PW + 128), b(15, LOC, PW + 128), b(LOC, PW),
            b(16, LOC, QW), b(HEADS, SLOTS, HD), b(SLOTS, QW + 128),
            b(16, LOC, QW + 128), b(16, LOC, QW + 128), b(16, LOC, QW),
            b(2, 64, WD), b(64, WD), b(4, 64, WD), b(4, 64, WD),
            f(1, 128), f(15, 1, 128),
            b(4, 4, CH, ROWS), b(4, 4, CH, ROWS),
            b(3, CH, ROWS), b(3, CH, ROWS), b(3, CH, ROWS), b(3, CH, ROWS),
            b(4, 3, CH, ROWS), b(4, 3, CH, ROWS),
            b(3, CH, ROWS), b(3, CH, ROWS), b(3, CH, ROWS), b(3, CH, ROWS),
            b(4, 4, CH, ROWS), f(ROWS, WD), f(HEADS * LOC, TAIL),
            pltpu.SemaphoreType.DMA((24,)),
            pltpu.SemaphoreType.DMA((N_SEM,)),
            pltpu.SemaphoreType.DMA((N_SEM,)),
        ],
        compiler_params=pltpu.CompilerParams(
            collective_id=0, has_side_effects=True, vmem_limit_bytes=56 * 1024 * 1024
        ),
        name="layer",
    )(x, gain1, wi, bias, wo, gain2, we, ws, pc, tc, tlen, idx, cnt)


def copies(x, cache, x_out, cache_out):
    x_out[...] = x[...]
    cache_out[...] = cache[...]


def write(x, cache):
    vmem = pl.BlockSpec(memory_space=pltpu.VMEM)
    return pl.pallas_call(
        copies,
        out_shape=[jax.ShapeDtypeStruct(x.shape, x.dtype), jax.ShapeDtypeStruct(cache.shape, cache.dtype)],
        in_specs=[vmem, vmem],
        out_specs=[vmem, vmem],
        name="write",
    )(x, cache)


def local(
    states, first_gain, input_weight, input_bias, output_weight, second_gain, expand_weight,
    shrink_weight, prompt_cache, tail_cache, tail_length, block_index, block_count,
):
    x, cache = layer(
        states.reshape(2, 64, WD),
        first_gain.reshape(1, WD),
        input_weight.reshape(WD, PW),
        input_bias.reshape(1, PW),
        output_weight.reshape(QW, WD),
        second_gain.reshape(1, WD),
        jnp.transpose(expand_weight, (1, 2, 0)),
        shrink_weight,
        prompt_cache.reshape(2, BLOCKS, BLOCK, HD),
        tail_cache.reshape(2, LOC, TAIL, HD),
        tail_length,
        jnp.transpose(block_index[:, 0], (0, 2, 1)),
        block_count,
    )
    x, cache = write(x, cache)
    cache = jnp.transpose(cache, (0, 2, 1, 3)).reshape(2, LOC, STEPS, 1, HD)
    return (x.reshape(ROWS, WD), cache)


def solution(mesh):
    return jax.shard_map(
        local,
        mesh=mesh,
        in_specs=(
            P(None, "kv"),
            P("kv"),
            P("kv", "tp", None),
            P("tp", None),
            P("tp", None, "kv"),
            P("kv"),
            P("kv", None, "tp"),
            P("tp", "kv"),
            P(None, "tp", "kv", None, None),
            P(None, "kv", None, "tp", None),
            P("kv"),
            P("kv", "tp", None, None),
            P("kv", "tp", None),
        ),
        out_specs=(P(None, "kv"), P(None, "kv", None, "tp", None)),
        check_vma=False,
    )
```

```python
import functools

import jax
import jax.numpy as jnp
from jax import lax
from jax.experimental import pallas as pl
from jax.experimental.pallas import tpu as pltpu
from jax.sharding import PartitionSpec as P

D = 8192
STEPS = 3
ROWS = 128
LOC = 8
HEADS = 8
HD = 128
QW = HEADS * HD
PW = QW + 2 * HD
BLOCKS = 16
BLOCK = 512
TAIL = 512
FF = 3696
CH = 240
FFP = 16 * CH
WD = 512
TILES = 32
PAIRS = 16
SLOTS = TILES * PAIRS
EPS = 1e-06
LOW = -1e30
SCALE = HD ** (-0.5)
SCALE2 = SCALE * 1.4426950408889634
VW = 2 * HD
F32 = jnp.float32
BF16 = jnp.bfloat16
MESH = pl.DeviceIdType.MESH

(TBL, RSP, AGQ, PART, AGO, TRA, TGA, SQR, TRB, TGB, G2, U2) = range(12)
A1, B1, A2, B2 = (12, 13, 14), (15, 16, 17), (18, 19, 20), (21, 22, 23)
G1, U1 = (24, 25, 26, 27), (28, 29, 30, 31)
RG, RU = (32, 33, 34), (35, 36, 37)
TA, TB = (TRA, TGA, 38), (TRB, TGB, 39)
N_SEM = 40
SUBS = ((0, 128), (128, CH - 128))
KV_ORDER = ((2, 2), (1, 2), (2, 1), (3, 2), (2, 3), (0, 2), (2, 0), (1, 1), (3, 3), (1, 3), (3, 1),
            (0, 1), (1, 0), (0, 3), (3, 0))
TP_ORDER = (4, 3, 5, 2, 6, 1, 7)


def nt(a, b):
    return lax.dot_general(a, b, (((1,), (1,)), ((), ())), preferred_element_type=F32)


def tn(a, b):
    return lax.dot_general(a, b, (((0,), (0,)), ((), ())), preferred_element_type=F32)


def mm(a, b):
    return jnp.dot(a, b, preferred_element_type=F32)


def split(v):
    hi = v.astype(BF16).astype(F32)
    lo = (v - hi).astype(BF16).astype(F32)
    return hi, lo


def kernel(
    x_hbm, gain1, wi_hbm, bias, wo_hbm, gain2, we_hbm, ws_hbm, pc_hbm, tc_hbm, tlen, idx, cnt,
    x_out, cache_out,
    xb, hb, wi, wo, wg, wu, ws, keys, vals, tail,
    table, tb, tsm, tvm, g01, gm, live01,
    ps, pr, pqkv, qall, qs, us, asend, arecv, oall,
    ys, sib, xra, xrb, sqs, sqr, gs, up, rlg, rlu, crg, cru, g1r, u1r, g1s, u1s, g2r, u2r, ug, acc, tlmask,
    wsem, ssem, rsem,
):
    me = lax.axis_index("kv")
    tp = lax.axis_index("tp")
    y = lax.div(me, 4)
    z = lax.rem(me, 4)

    def kv_at(dy, dz):
        return lax.rem(y + dy, 4) * 4 + lax.rem(z + dz, 4)

    def send(src, dst, ph, to_kv, to_tp):
        pltpu.make_async_remote_copy(
            src_ref=src, dst_ref=dst, send_sem=ssem.at[ph], recv_sem=rsem.at[ph],
            device_id=(to_kv, to_tp), device_id_type=MESH,
        ).start()

    def got(ref, ph):
        pltpu.make_async_copy(ref, ref, rsem.at[ph]).wait()

    def sent(ref, ph):
        pltpu.make_async_copy(ref, ref, ssem.at[ph]).wait()

    def to_all_kv(fn):
        for dy, dz in KV_ORDER:
            fn(4 * dy + dz, kv_at(dy, dz))

    def to_all_tp(fn):
        for d in TP_ORDER:
            fn(d, lax.rem(tp + d, 8))

    barrier = pltpu.get_barrier_semaphore()
    to_all_kv(lambda d, dst: pl.semaphore_signal(
        barrier, inc=1, device_id=(dst, tp), device_id_type=MESH))
    to_all_tp(lambda d, dst: pl.semaphore_signal(
        barrier, inc=1, device_id=(me, dst), device_id_type=MESH))

    def up_rows(i):
        n = min(CH, FF - i * CH)
        return pltpu.make_async_copy(
            we_hbm.at[1, pl.ds(i * CH, n)], wu.at[i % 4, i // 4, pl.ds(0, n)], wsem.at[8 + i])

    loads = [
        pltpu.make_async_copy(x_hbm, xb, wsem.at[0]),
        pltpu.make_async_copy(wi_hbm, wi, wsem.at[1]),
        pltpu.make_async_copy(tc_hbm, tail, wsem.at[2]),
        pltpu.make_async_copy(pc_hbm.at[0], keys, wsem.at[3]),
        pltpu.make_async_copy(pc_hbm.at[1], vals.at[:, :, pl.ds(0, HD)], wsem.at[4]),
        pltpu.make_async_copy(wo_hbm, wo, wsem.at[5]),
        pltpu.make_async_copy(we_hbm.at[0], wg.at[pl.ds(0, FF)], wsem.at[6]),
        pltpu.make_async_copy(ws_hbm, ws.at[pl.ds(0, FF)], wsem.at[7]),
    ]
    ups = [up_rows(i) for i in range(16)]
    for load in loads + ups:
        load.start()

    table[...] = jnp.zeros_like(table)
    table[:, 0:16] = idx[:, 0, :]
    table[:, 16:32] = idx[:, 1, :]
    table[:, 32:48] = cnt[:, 0, :]
    tb[me] = table[...]

    def project():
        xf = xb[...].astype(F32).reshape(ROWS, WD)
        sq = jnp.sum(xf * xf, axis=1, keepdims=True)
        a = (xf * gain1[...]).astype(BF16)
        ps[:, :, 0:PW] = mm(a, wi[...]).reshape(16, LOC, PW).astype(BF16)
        hi, lo = split(sq)
        half = lax.broadcasted_iota(jnp.int32, (ROWS, 128), 1) < 64
        ps[:, :, PW:PW + 128] = jnp.where(half, hi, lo).reshape(16, LOC, 128).astype(BF16)

    wg[FF:FFP, :] = jnp.zeros((FFP - FF, WD), BF16)
    wu[3, 3, FF - 15 * CH:CH, :] = jnp.zeros((FFP - FF, WD), BF16)
    vals[:, :, HD:VW] = jnp.ones((BLOCKS, BLOCK, HD), BF16)
    ws[FF:FFP, :] = jnp.zeros((FFP - FF, WD), BF16)
    cache_out[...] = jnp.zeros_like(cache_out)
    rowmod = lax.rem(lax.broadcasted_iota(jnp.int32, (HEADS * LOC, TAIL), 0), LOC)
    tlm = jnp.zeros((HEADS * LOC, TAIL), jnp.int32)
    for r in range(LOC):
        tlm = jnp.where(rowmod == r, tlen[r], tlm)
    tpos = lax.broadcasted_iota(jnp.int32, (HEADS * LOC, TAIL), 1)
    tlmask[...] = (tpos < tlm).astype(F32)

    loads[0].wait()
    loads[1].wait()
    project()
    pl.semaphore_wait(barrier, 22)

    def sort_pairs():
        lane = lax.broadcasted_iota(jnp.int32, (ROWS, 128), 1)
        row = lax.broadcasted_iota(jnp.int32, (ROWS, 128), 0)
        valid = lane < BLOCKS
        b0, b1, n = [
            jnp.sum(jnp.where(lane == me + 16 * k, tb[...].reshape(ROWS, 128).astype(F32), 0.0),
                    axis=1, keepdims=True).astype(jnp.int32) for k in range(3)
        ]
        e0 = jnp.where((b0 == lane) & (n > 0) & valid, 1.0, 0.0).astype(F32)
        e1 = jnp.where((b1 == lane) & (n > 1) & valid, 1.0, 0.0).astype(F32)
        lower = jnp.where(lane < row, 1.0, 0.0).astype(BF16)
        c0 = mm(lower, e0.astype(BF16))
        c1 = mm(lower, e1.astype(BF16))
        n0 = jnp.sum(e0, axis=0, keepdims=True)
        n1 = jnp.sum(e1, axis=0, keepdims=True)
        n = (n0 + n1).astype(jnp.int32)
        ntile = lax.shift_right_logical(n + (PAIRS - 1), 4).astype(F32)
        upper = jnp.where(row < lane, 1.0, 0.0).astype(BF16)
        nt8 = jnp.broadcast_to(ntile, (8, 128))
        tstart = mm(nt8.astype(BF16), upper)[0:1]
        p0 = jnp.sum(e0 * (PAIRS * tstart + c0), axis=1, keepdims=True)
        p1 = jnp.sum(e1 * (PAIRS * tstart + n0 + c1), axis=1, keepdims=True)
        l0 = jnp.sum(e0, axis=1, keepdims=True)
        l1 = jnp.sum(e1, axis=1, keepdims=True)
        p0 = jnp.where(l0 > 0.5, p0, -1.0).astype(jnp.int32)
        p1 = jnp.where(l1 > 0.5, p1, -1.0).astype(jnp.int32)
        live01[0] = jnp.broadcast_to(l0, (ROWS, 128))
        live01[1] = jnp.broadcast_to(l1, (ROWS, 128))
        slot = lax.broadcasted_iota(jnp.int32, (ROWS, SLOTS), 1)
        h0 = jnp.where(p0 == slot, 1.0, 0.0).astype(F32)
        h1 = jnp.where(p1 == slot, 1.0, 0.0).astype(F32)
        g01[0:ROWS] = h0.astype(BF16)
        g01[ROWS:2 * ROWS] = h1.astype(BF16)
        gm[...] = (h0 + h1).T.astype(BF16)
        tend = tstart + ntile
        ti = lax.broadcasted_iota(jnp.int32, (TILES, 128), 0).astype(F32)
        tl = lax.broadcasted_iota(jnp.int32, (TILES, 128), 1)
        done = jnp.where((tl < BLOCKS) & (tend <= ti), 1.0, 0.0).astype(F32)
        cnt = jnp.minimum(jnp.sum(done, axis=1, keepdims=True), BLOCKS - 1.0)
        tvm[...] = jnp.broadcast_to(cnt, (TILES, 128)).astype(jnp.int32)
        pltpu.sync_copy(tvm, tsm)

    core = lax.rem(tp, 2)
    chip = lax.div(tp, 2)
    sibling = tp + 1 - 2 * core

    def tp_sum(part, ph, xr, res, dst):
        ys[...] = part.reshape(2, 64, WD).astype(BF16)
        send(ys.at[1 - core], sib, ph[0], me, sibling)
        own = ys[core].astype(F32)
        got(sib, ph[0])
        xr[chip] = (own + sib[...].astype(F32)).astype(BF16)
        for d in (2, 1, 3):
            send(xr.at[chip], xr.at[chip], ph[1], me, lax.rem(tp + 2 * d, 8))
        sent(sib, ph[0])
        got(xr.at[pl.ds(0, 3)], ph[1])
        total = xr[0].astype(F32)
        for d in range(1, 4):
            total = total + xr[d].astype(F32)
        dst[core] = (res[core].astype(F32) + total.astype(BF16).astype(F32)).astype(BF16)
        send(dst.at[core], dst.at[core], ph[2], me, sibling)
        sent(xr.at[pl.ds(0, 3)], ph[1])
        got(dst.at[0], ph[2])

    def step(s, carry):
        to_all_kv(lambda d, dst: send(ps.at[dst], pr.at[d - 1], RSP, dst, tp))

        @pl.when(s == 0)
        def _():
            to_all_kv(lambda d, dst: send(table, tb.at[me], TBL, dst, tp))

        @pl.when(s > 0)
        def _():
            sent(xb.at[0], TB[2])


        total = ps[me].astype(F32)
        got(pr, RSP)
        for d in range(15):
            total = total + pr[d].astype(F32)
        factor = lax.rsqrt((total[:, PW:PW + 1] + total[:, PW + 64:PW + 65]) / D + EPS)
        proj = (total[:, 0:PW] * factor + bias[...].astype(F32)).astype(BF16)
        pqkv[...] = proj
        cache_out[0, s] = proj[:, QW:QW + HD]
        cache_out[1, s] = proj[:, QW + HD:QW + 2 * HD]
        qall[me] = proj[:, 0:QW]
        to_all_kv(lambda d, dst: send(qall.at[me], qall.at[me], AGQ, dst, tp))
        sent(pr, RSP)

        @pl.when(s == 0)
        def _():
            got(tb.at[pl.ds(0, 15)], TBL)
            sent(tb.at[pl.ds(0, 15)], TBL)
            sort_pairs()
            loads[2].wait()

        pf = pqkv[...].astype(F32)
        qh = jnp.concatenate([pf[:, h * HD:(h + 1) * HD] for h in range(HEADS)], axis=0)
        qhb = qh.astype(BF16)
        rm = lax.rem(lax.broadcasted_iota(jnp.int32, (HEADS * LOC, TAIL), 0), LOC)
        sc = jnp.zeros((HEADS * LOC, TAIL), F32)
        for r in range(LOC):
            sc = jnp.where(rm == r, nt(qhb, tail[0, r]), sc)
        sc = sc * SCALE2
        tmask = tlmask[...] > 0.5
        sc = jnp.where(tmask, sc, LOW)
        fresh = []
        for t in range(STEPS):
            kf = cache_out[0, t].astype(F32)
            kf = jnp.concatenate([kf] * HEADS, axis=0)
            f = jnp.sum(qh * kf, axis=1, keepdims=True) * SCALE2
            fresh.append(jnp.where(t <= s, f, LOW))
        tm = jnp.max(sc, axis=1, keepdims=True)
        for f in fresh:
            tm = jnp.maximum(tm, f)
        e = jnp.where(tmask, jnp.exp2(sc - tm), 0.0)
        tl = jnp.sum(e, axis=1, keepdims=True)
        eb = e.astype(BF16)
        tu = jnp.zeros((HEADS * LOC, HD), F32)
        for r in range(LOC):
            tu = tu + mm(jnp.where(rm == r, eb, jnp.zeros_like(eb)), tail[1, r])
        for t in range(STEPS):
            ef = jnp.where(t <= s, jnp.exp2(fresh[t] - tm), 0.0)
            tl = tl + ef
            vf = cache_out[1, t].astype(F32)
            tu = tu + ef.astype(BF16).astype(F32) * jnp.concatenate([vf] * HEADS, axis=0)

        got(qall.at[pl.ds(0, 15)], AGQ)
        for h in range(0, HEADS, 2):
            qa = qall[:, :, h * HD:(h + 2) * HD].astype(F32).reshape(ROWS, 2 * HD).astype(BF16)
            both = mm(gm[...], qa).astype(BF16)
            qs[h] = both[:, 0:HD]
            qs[h + 1] = both[:, HD:2 * HD]

        @pl.when(s == 0)
        def _():
            loads[3].wait()
            loads[4].wait()

        lane16 = lax.broadcasted_iota(jnp.int32, (PAIRS, 128), 1)

        def tile(t, c):
            b = jnp.minimum(jnp.maximum(tsm[t, 0], 0), BLOCKS - 1)
            at = pl.ds(pl.multiple_of(t * PAIRS, PAIRS), PAIRS)
            q = jnp.concatenate([qs[h, at, :] for h in range(HEADS)], axis=0)
            sc = nt(keys[b], q) * SCALE2
            mh, ml = split(jnp.max(sc, axis=0, keepdims=True))
            m = mh + ml
            e = jnp.exp2(sc - m)
            u = tn(e.astype(BF16), vals[b])
            mt = jnp.broadcast_to(m, (128, 128)).T
            info = jnp.zeros((PAIRS, 128), F32)
            for h in range(HEADS):
                rows = slice(h * PAIRS, (h + 1) * PAIRS)
                us[at, h * HD:(h + 1) * HD] = u[rows, 0:HD].astype(BF16)
                info = jnp.where(lane16 == h, mt[rows], info)
                info = jnp.where(lane16 == 8 + h, u[rows, HD:VW], info)
            hi, lo = split(info)
            us[at, QW:QW + 128] = (hi + pltpu.roll(lo, 16, 1)).astype(BF16)
            return c

        lax.fori_loop(0, TILES, tile, 0, unroll=32)

        lane = lax.broadcasted_iota(jnp.int32, (ROWS, 128), 1)
        head = lane < HEADS
        info = mm(g01[...], us[:, QW:QW + 128])
        m01, l01 = [], []
        for c in range(2):
            f = info[c * ROWS:(c + 1) * ROWS]
            f = f + pltpu.roll(f, 112, 1)
            m01.append(jnp.where(head & (live01[c] > 0.5), f, LOW))
            l01.append(pltpu.roll(f, 120, 1))
        m = jnp.maximum(m01[0], m01[1])
        w01 = [jnp.where(head & (live01[c] > 0.5), jnp.exp2(m01[c] - m), 0.0) for c in range(2)]
        l = jnp.where(head, w01[0] * l01[0] + w01[1] * l01[1], 0.0)
        hi, lo = split(jnp.where(head, m, 0.0) + pltpu.roll(l, 8, 1))
        packed = hi + pltpu.roll(lo, 16, 1)
        asend[:, :, QW:QW + 128] = packed.reshape(16, LOC, 128).astype(BF16)
        for h in range(0, HEADS, 2):
            both = mm(g01[...], us[:, h * HD:(h + 2) * HD])
            for k in range(2):
                cols = slice(k * HD, (k + 1) * HD)
                at = slice((h + k) * HD, (h + k + 1) * HD)
                u = both[0:ROWS, cols] * w01[0][:, h + k:h + k + 1]
                u = u + both[ROWS:, cols] * w01[1][:, h + k:h + k + 1]
                asend[:, :, at] = u.reshape(16, LOC, HD).astype(BF16)
        to_all_kv(lambda d, dst: send(asend.at[dst], arecv.at[d - 1], PART, dst, tp))
        sent(qall.at[pl.ds(0, 15)], AGQ)

        lane8 = lax.broadcasted_iota(jnp.int32, (LOC, 128), 1)
        head8 = lane8 < HEADS
        tmc = jnp.full((LOC, 128), LOW, F32)
        tlc = jnp.zeros((LOC, 128), F32)
        for h in range(HEADS):
            tmc = jnp.where(lane8 == h, tm[h * LOC:(h + 1) * LOC], tmc)
            tlc = jnp.where(lane8 == h, tl[h * LOC:(h + 1) * LOC], tlc)
        arecv[15] = asend[me]
        got(arecv.at[pl.ds(0, 15)], PART)
        ms, lsum = [], []
        top = tmc
        for o in range(16):
            f = arecv[o, :, QW:QW + 128].astype(F32)
            f = f + pltpu.roll(f, 112, 1)
            m = jnp.where(head8, f, LOW)
            ms.append(m)
            lsum.append(pltpu.roll(f, 120, 1))
            top = jnp.maximum(top, m)
        wt = jnp.exp2(tmc - top)
        wo_ = [jnp.exp2(m - top) for m in ms]
        den = wt * tlc
        for o in range(16):
            den = den + wo_[o] * lsum[o]
        inv = jnp.where(head8, 1.0 / jnp.where(head8, den, 1.0), 0.0)
        wt = wt * inv
        wo_ = [w * inv for w in wo_]
        for h in range(HEADS):
            o_h = wt[:, h:h + 1] * tu[h * LOC:(h + 1) * LOC]
            for o in range(16):
                o_h = o_h + wo_[o][:, h:h + 1] * arecv[o, :, h * HD:(h + 1) * HD].astype(F32)
            oall[me, :, h * HD:(h + 1) * HD] = o_h.astype(BF16)
        to_all_kv(lambda d, dst: send(oall.at[me], oall.at[me], AGO, dst, tp))
        sent(arecv.at[pl.ds(0, 15)], PART)

        @pl.when(s == 0)
        def _():
            loads[5].wait()

        got(oall.at[pl.ds(0, 15)], AGO)
        oa = oall[...].astype(F32).reshape(ROWS, QW).astype(BF16)
        tp_sum(mm(oa, wo[...]), TA, xra, xb, hb)

        hf = hb[...].astype(F32).reshape(ROWS, WD)
        a2 = (hf * gain2[...]).astype(BF16)

        @pl.when(s == 0)
        def _():
            loads[6].wait()
            for load in ups:
                load.wait()

        subs = [pl.ds(*sub) for sub in SUBS]
        lo, hi = subs
        yp, ym, zp, zm = [lax.rem(v + k, 4) for v in (y, z) for k in (1, 3)]
        y2, z2 = lax.rem(y + 2, 4), lax.rem(z + 2, 4)

        def at_y(t):
            return t * 4 + z

        def at_z(t):
            return y * 4 + t

        for off in (2, 1, 3, 0):
            yk = lax.rem(y + off, 4)
            zk = lax.rem(z + off, 4)
            rows = pl.ds(pl.multiple_of(yk * (4 * CH), 16), 4 * CH)
            for own, there, into, relay, sem, rsm, dev, far, plus, minus in (
                (gs, yk, g1r, rlg, G1, RG, at_z, z2, zp, zm),
                (up, zk, u1r, rlu, U1, RU, at_y, y2, yp, ym),
            ):
                w = wg[rows, :] if own is gs else wu[zk].reshape(4 * CH, WD)
                own[there] = nt(w, a2).reshape(4, CH, ROWS).astype(BF16)
                if off > 0:
                    e = off - 1
                    send(own.at[there, far, lo], relay.at[e, lo], rsm[e], dev(plus), tp)
                    send(own.at[there, far, hi], relay.at[e, hi], rsm[e], dev(minus), tp)
                    send(own.at[there, plus, hi], into.at[off, 0, hi], sem[off], dev(plus), tp)
                    send(own.at[there, minus, lo], into.at[off, 2, lo], sem[off], dev(minus), tp)
                else:
                    for k, t in ((2, far), (1, plus), (3, minus)):
                        send(own.at[there, t], into.at[0, k - 1], sem[0], dev(t), tp)
            if off == 2:
                sent(oall.at[pl.ds(0, 15)], AGO)
                sent(hb.at[0], TA[2])
                sq = jnp.sum(hf * hf, axis=1, keepdims=True)
                sqs[...] = jnp.broadcast_to(sq, (ROWS, 128)).T[0:1]
                to_all_kv(lambda d, dst: send(sqs, sqr.at[d - 1], SQR, dst, tp))
        for off in (2, 1, 3):
            yk = lax.rem(y + off, 4)
            zk = lax.rem(z + off, 4)
            e = off - 1
            for own, there, into, relay, both, sem, rsm, dev, plus, minus in (
                (gs, yk, g1r, rlg, crg, G1, RG, at_z, zp, zm),
                (up, zk, u1r, rlu, cru, U1, RU, at_y, yp, ym),
            ):
                got(relay.at[e], rsm[e])
                v = own[there, plus, lo, :].astype(F32) + relay[e, lo, :].astype(F32)
                both[e, lo, :] = v.astype(BF16)
                send(both.at[e, lo], into.at[off, 0, lo], sem[off], dev(plus), tp)
                v = own[there, minus, hi, :].astype(F32) + relay[e, hi, :].astype(F32)
                both[e, hi, :] = v.astype(BF16)
                send(both.at[e, hi], into.at[off, 2, hi], sem[off], dev(minus), tp)
        for off in (2, 1, 3, 0):
            yk = lax.rem(y + off, 4)
            zk = lax.rem(z + off, 4)
            parts = (0, 2) if off > 0 else (0, 1, 2)
            got(g1r.at[off, pl.ds(0, len(parts))], G1[off])
            gate = gs[yk, z].astype(F32)
            for d in parts:
                gate = gate + g1r[off, d].astype(F32)
            if off > 0:
                g1s[off - 1] = gate.astype(BF16)
                send(g1s.at[off - 1], g2r.at[off - 1], G2, at_y(yk), tp)
            got(u1r.at[off, pl.ds(0, len(parts))], U1[off])
            upv = up[zk, y].astype(F32)
            for d in parts:
                upv = upv + u1r[off, d].astype(F32)
            if off > 0:
                u1s[off - 1] = upv.astype(BF16)
                send(u1s.at[off - 1], u2r.at[off - 1], U2, at_z(zk), tp)
        got(sqr, SQR)
        sqt = sqs[...]
        for d in range(15):
            sqt = sqt + sqr[d]
        factor = lax.rsqrt(sqt / D + EPS)[0:1]
        got(g2r, G2)
        got(u2r, U2)
        for d in range(3):
            gate = gate + g2r[d].astype(F32)
            upv = upv + u2r[d].astype(F32)
        gate = gate * factor
        upv = upv * factor
        ug[y, z] = (gate / (1.0 + jnp.exp(-gate)) * upv).astype(BF16)

        first, second = ug.at[y, z, subs[0]], ug.at[y, z, subs[1]]
        for k in (2, 1, 3):
            send(first, first, A1[k - 1], lax.rem(y + k, 4) * 4 + z, tp)
            send(second, second, B1[k - 1], y * 4 + lax.rem(z + k, 4), tp)
        for k in (2, 1, 3):
            send(first, first, A2[k - 1], y * 4 + lax.rem(z + k, 4), tp)
            send(second, second, B2[k - 1], lax.rem(y + k, 4) * 4 + z, tp)
        for d in (1, 3, 2):
            slab = ug.at[lax.rem(y + 4 - d, 4), z, subs[0]]
            got(slab, A1[d - 1])
            for k in (2, 1, 3):
                send(slab, slab, A2[k - 1], y * 4 + lax.rem(z + k, 4), tp)
            slab = ug.at[y, lax.rem(z + 4 - d, 4), subs[1]]
            got(slab, B1[d - 1])
            for k in (2, 1, 3):
                send(slab, slab, B2[k - 1], lax.rem(y + k, 4) * 4 + z, tp)
        sent(sqr, SQR)
        for off in range(4):
            n = 3 if off == 0 else 2
            sent(g1r.at[off, pl.ds(0, n)], G1[off])
            sent(u1r.at[off, pl.ds(0, n)], U1[off])
        for e in range(3):
            sent(rlg.at[e], RG[e])
            sent(rlu.at[e], RU[e])
        sent(g2r, G2)
        sent(u2r, U2)

        @pl.when(s == 0)
        def _():
            loads[7].wait()

        def down(c, at):
            lo, n = SUBS[c]
            spots = [(t, at) if c == 0 else (at, t) for t in range(4)]
            u = [ug[i, j, lo:lo + n, :] for i, j in spots]
            w = [ws[pl.ds(pl.multiple_of((i * 4 + j) * CH + lo, 16), n), :] for i, j in spots]
            return mm(jnp.concatenate(u, axis=0).T, jnp.concatenate(w, axis=0))

        acc[...] = down(0, z)
        acc[...] += down(1, y)
        for d in (1, 3, 2):
            got(ug.at[:, 0, subs[0]], A2[d - 1])
            acc[...] += down(0, lax.rem(z + 4 - d, 4))
            got(ug.at[0, :, subs[1]], B2[d - 1])
            acc[...] += down(1, lax.rem(y + 4 - d, 4))
        for d in range(3):
            sent(first, A1[d])
            sent(second, B1[d])
            sent(ug.at[:, 0, subs[0]], A2[d])
            sent(ug.at[0, :, subs[1]], B2[d])
        tp_sum(acc[...], TB, xrb, hb, xb)

        @pl.when(s < STEPS - 1)
        def _():
            project()

        return carry

    lax.fori_loop(0, STEPS, step, 0)
    sent(xb.at[0], TB[2])
    x_out[...] = xb[...]


def layer(x, gain1, wi, bias, wo, gain2, we, ws, pc, tc, tlen, idx, cnt):
    vmem = pl.BlockSpec(memory_space=pltpu.VMEM)
    smem = pl.BlockSpec(memory_space=pltpu.SMEM)
    hbm = pl.BlockSpec(memory_space=pl.ANY)
    b = lambda *shape: pltpu.VMEM(shape, BF16)
    f = lambda *shape: pltpu.VMEM(shape, F32)
    i = lambda *shape: pltpu.VMEM(shape, jnp.int32)
    return pl.pallas_call(
        kernel,
        out_shape=[
            jax.ShapeDtypeStruct((2, 64, WD), BF16),
            jax.ShapeDtypeStruct((2, STEPS, LOC, HD), BF16),
        ],
        in_specs=[hbm, vmem, hbm, vmem, hbm, vmem, hbm, hbm, hbm, hbm, smem, vmem, vmem],
        out_specs=[vmem, vmem],
        scratch_shapes=[
            b(2, 64, WD), b(2, 64, WD),
            b(WD, PW), b(QW, WD), b(FFP, WD), b(4, 4, CH, WD), b(FFP, WD),
            b(BLOCKS, BLOCK, HD), b(BLOCKS, BLOCK, VW), b(2, LOC, TAIL, HD),
            i(LOC, 128), i(16, LOC, 128), pltpu.SMEM((TILES, 128), jnp.int32), i(TILES, 128),
            b(2 * ROWS, SLOTS), b(SLOTS, ROWS), f(2, ROWS, 128),
            b(16, LOC, PW + 128), b(15, LOC, PW + 128), b(LOC, PW),
            b(16, LOC, QW), b(HEADS, SLOTS, HD), b(SLOTS, QW + 128),
            b(16, LOC, QW + 128), b(16, LOC, QW + 128), b(16, LOC, QW),
            b(2, 64, WD), b(64, WD), b(4, 64, WD), b(4, 64, WD),
            f(1, 128), f(15, 1, 128),
            b(4, 4, CH, ROWS), b(4, 4, CH, ROWS),
            b(3, CH, ROWS), b(3, CH, ROWS), b(3, CH, ROWS), b(3, CH, ROWS),
            b(4, 3, CH, ROWS), b(4, 3, CH, ROWS),
            b(3, CH, ROWS), b(3, CH, ROWS), b(3, CH, ROWS), b(3, CH, ROWS),
            b(4, 4, CH, ROWS), f(ROWS, WD), f(HEADS * LOC, TAIL),
            pltpu.SemaphoreType.DMA((24,)),
            pltpu.SemaphoreType.DMA((N_SEM,)),
            pltpu.SemaphoreType.DMA((N_SEM,)),
        ],
        compiler_params=pltpu.CompilerParams(
            collective_id=0, has_side_effects=True, vmem_limit_bytes=56 * 1024 * 1024
        ),
        name="layer",
    )(x, gain1, wi, bias, wo, gain2, we, ws, pc, tc, tlen, idx, cnt)


def copies(x, cache, x_out, cache_out):
    x_out[...] = x[...]
    cache_out[...] = cache[...]


def write(x, cache):
    vmem = pl.BlockSpec(memory_space=pltpu.VMEM)
    return pl.pallas_call(
        copies,
        out_shape=[jax.ShapeDtypeStruct(x.shape, x.dtype), jax.ShapeDtypeStruct(cache.shape, cache.dtype)],
        in_specs=[vmem, vmem],
        out_specs=[vmem, vmem],
        name="write",
    )(x, cache)


def local(
    states, first_gain, input_weight, input_bias, output_weight, second_gain, expand_weight,
    shrink_weight, prompt_cache, tail_cache, tail_length, block_index, block_count,
):
    x, cache = layer(
        states.reshape(2, 64, WD),
        first_gain.reshape(1, WD),
        input_weight.reshape(WD, PW),
        input_bias.reshape(1, PW),
        output_weight.reshape(QW, WD),
        second_gain.reshape(1, WD),
        jnp.transpose(expand_weight, (1, 2, 0)),
        shrink_weight,
        prompt_cache.reshape(2, BLOCKS, BLOCK, HD),
        tail_cache.reshape(2, LOC, TAIL, HD),
        tail_length,
        jnp.transpose(block_index[:, 0], (0, 2, 1)),
        block_count,
    )
    x, cache = write(x, cache)
    cache = jnp.transpose(cache, (0, 2, 1, 3)).reshape(2, LOC, STEPS, 1, HD)
    return (x.reshape(ROWS, WD), cache)


def solution(mesh):
    return jax.shard_map(
        local,
        mesh=mesh,
        in_specs=(
            P(None, "kv"),
            P("kv"),
            P("kv", "tp", None),
            P("tp", None),
            P("tp", None, "kv"),
            P("kv"),
            P("kv", None, "tp"),
            P("tp", "kv"),
            P(None, "tp", "kv", None, None),
            P(None, "kv", None, "tp", None),
            P("kv"),
            P("kv", "tp", None, None),
            P("kv", "tp", None),
        ),
        out_specs=(P(None, "kv"), P(None, "kv", None, "tp", None)),
        check_vma=False,
    )
```
